128 devices in a mesh: node: 8 (over z, core), local: 16 (over x, y).
Axes of the slice: x: 4, y: 4, z: 4, core: 2. Of those that a mesh axis runs over, the one named last changes fastest.
Arguments:
- latent: bfloat16 [16384, 1024], P(('node', 'local')), may hold values from -6 to 6
- grad_out: bfloat16 [16384, 1024], P(('node', 'local')), may hold values from -6 to 6
- expert_ids: int32 [16384, 4], P(('node', 'local')), may hold values from 0 to 127, all different within a row; in each aligned block of 128 rows (0 to 127, 128 to 255, ...) at most 6 rows name the same one
- combine: bfloat16 [16384, 4], P(('node', 'local')), may hold values from 0.099609375 to 0.59765625
- w_up: bfloat16 [128, 2, 1024, 1344], P(('node', 'local')), may hold values from -0.1875 to 0.1875
- w_down: bfloat16 [128, 2, 1344, 1024], P(('node', 'local')), may hold values from -0.125 to 0.125
Outputs:
- d_latent: bfloat16 [16384, 1024], P(('node', 'local'))
- d_combine: float32 [16384, 4], P(('node', 'local'))
- d_up: bfloat16 [128, 2, 1024, 1344], P(('node', 'local'))
- d_down: bfloat16 [128, 2, 1344, 1024], P(('node', 'local'))
The draws below stay inside these ranges and needn't reach their ends.
Inputs may be any that keep to these rules, and one draw needn't show every extreme that they name: `expert_ids`: each row names 4 different experts. Within the rows of one device (aligned blocks of 128 rows) no expert is named by more than 6 rows, a bound that some block reaches.
All inputs are finite; a program needn't handle non-finite values.
Results may differ from the reference program's by a relative error of at most 0.005.
Values may be sent and summed in bfloat16 or wider, within the bound.
No kernel may reach another device: no remote copies, remote signals or barrier semaphores. Data moves between devices by JAX's collectives and lax.ppermute only.
A program may use at most 192 MiB of HBM per device.

```python
import math
import jax
import jax.numpy as jnp
import numpy as np
from jax import lax

LATENT = 1024
HIDDEN_SIZE = 2688
TOPK = 4
EXP_DEV = 2
TOK_DEV = 128
FH = 1344
OWNERS = 128
EXPERTS = 128
TOKENS = 16384
CAP = 6


def block_levels(own_key, dims, cuts, smallest, largest):
    gain, own = 1.0, jax.random.fold_in(own_key, 6)
    for axis_at, blocks in cuts:
        steps = jnp.exp(jax.random.uniform(jax.random.fold_in(own, axis_at), (blocks,), jnp.float32, smallest / len(cuts), largest / len(cuts)))
        gain = gain * jnp.repeat(steps, dims[axis_at] // blocks).reshape([-1 if axis == axis_at else 1 for axis in range(len(dims))])
    return gain


def shared_out(rng, own, number, rows, count, top, most, lean):
    sequence = jax.random.permutation(rng, count)
    crowded, common = load_shares(count, rows * top, most, lean, True), load_shares(count, rows * top, most, lean, False)
    places = jnp.arange(count)

    def named(tallies, offset_by):
        used = int((tallies > 0).sum())
        fixed = max(1, used // 4)
        moved = fixed + (places - fixed + offset_by * (used - fixed)) % max(1, count - fixed)
        return jnp.zeros((count,), jnp.int32).at[sequence[jnp.where(places < fixed, places, moved)]].set(jnp.asarray(tallies, jnp.int32))

    tallies = jnp.where(number % 4 == 0, named(crowded, number // 4), named(common, number - number // 4 - 1))
    mixed = jax.random.permutation(jax.random.fold_in(own, 3), count)
    source_of, sink = mixed[0:count // 2 * 2:2], mixed[1:count // 2 * 2:2]
    slack = jnp.minimum(tallies[source_of] - 1, most - tallies[sink]) // 2
    slack = jnp.where((source_of == sequence[0]) | (sink == sequence[0]) | (tallies[sink] == 0), 0, jnp.maximum(slack, 0))
    moved = jax.random.randint(jax.random.fold_in(own, 4), (count // 2,), 0, 1 << 20) % (slack + 1)
    tallies = tallies.at[source_of].add(-moved).at[sink].add(moved)
    members = jnp.searchsorted(jnp.cumsum(tallies), jnp.arange(rows * top), side="right").astype(jnp.int32)
    listing = members.reshape(top, rows).T
    listing = listing[jax.random.permutation(jax.random.fold_in(own, 1), rows)]
    offset_by = jax.random.randint(jax.random.fold_in(own, 2), (rows, 1), 0, top)
    return jnp.take_along_axis(listing, (jnp.arange(top)[None, :] + offset_by) % top, axis=1)


def load_shares(number_of, total, reach, skew, full):
    portions = [(1 << 20) // math.isqrt(standing ** skew) + 1 for standing in range(1, number_of + 1)]
    largest = reach if full else min(reach, max(-(-total // number_of), total * portions[0] // sum(portions)))
    least = 1 if total - largest >= number_of - 1 else 0
    given, surplus = [largest] + [least] * (number_of - 1), total - largest - least * (number_of - 1)
    while surplus > 0:
        movable = [i for i in range(1, number_of) if given[i] < largest] or [i for i in range(1, number_of) if given[i] < reach]
        mass, budget = sum([portions[i] for i in movable]), surplus
        for i in movable:
            more = min(reach - given[i], max(1, budget * portions[i] // mass), surplus)
            given[i] = given[i] + more
            surplus = surplus - more
    return np.array(given)


def normal_values(stream_key, extent, spread, reach, split=(), kind=jnp.bfloat16):
    gain = block_levels(stream_key, extent, split, -0.22, 0.18) if split else 1.0
    drawn = jax.random.normal(stream_key, extent, jnp.float32) * spread * gain
    return jnp.minimum(jnp.maximum(drawn, -reach), reach).astype(kind)


def setup_inputs(seed: int = 0) -> dict:
    keys = jax.random.split(jax.random.key(seed), 7)
    latent = normal_values(keys[0], (TOKENS, LATENT), 1.0, 6.0, ((0, 128),))
    grad_out = normal_values(keys[1], (TOKENS, LATENT), 1.0, 6.0, ((0, 128),))
    expert_ids_keys = jax.random.split(jax.random.fold_in(keys[2], 1), TOKENS // TOK_DEV)
    expert_ids_turns = jax.random.permutation(jax.random.fold_in(keys[2], 3), TOKENS // TOK_DEV)
    expert_ids = jax.vmap(lambda own, number: shared_out(jax.random.fold_in(keys[2], 2), own, number, TOK_DEV, EXPERTS, TOPK, CAP, 0))(expert_ids_keys, expert_ids_turns).reshape((TOKENS, TOPK))
    combine = jnp.clip(0.099609375 + 0.49804688 * jax.random.uniform(keys[3], (TOKENS, TOPK), jnp.float32) ** block_levels(keys[3], (TOKENS, TOPK), ((0, 128),), -0.2, 0.2), 0.099609375, 0.59765625).astype(jnp.bfloat16)
    w_up = normal_values(keys[4], (OWNERS, EXP_DEV, LATENT, FH), LATENT ** -0.5, 0.1875, ((0, 128),))
    w_down = normal_values(keys[5], (OWNERS, EXP_DEV, FH, LATENT), HIDDEN_SIZE ** -0.5, 0.125, ((0, 128),))
    return dict(latent=latent, grad_out=grad_out, expert_ids=expert_ids, combine=combine, w_up=w_up, w_down=w_down)


def block_ranks(id_rows, count):
    onehot = (id_rows[..., None] == jnp.arange(count, dtype=jnp.int32)).astype(jnp.int32)
    before = jnp.cumsum(onehot, axis=-2) - onehot
    return jnp.sum(before * onehot, axis=-1)


def expert_backward(rows_in, rows_grad, rows_mix, upper, lower):
    pre = jnp.dot(rows_in, upper, preferred_element_type=jnp.float32)
    active = jnp.maximum(pre, 0.0)
    squared = active * active
    pulled = lax.dot_general(rows_grad, lower, (((1,), (1,)), ((), ())), preferred_element_type=jnp.float32)
    mixing = rows_mix.astype(jnp.float32)[:, None]
    mix_grad = jnp.sum(squared * pulled, axis=1)
    hidden_grad = (2.0 * mixing * pulled * active).astype(jnp.bfloat16)
    input_grad = lax.dot_general(hidden_grad, upper, (((1,), (1,)), ((), ())), preferred_element_type=jnp.float32)
    upper_grad = lax.dot_general(rows_in, hidden_grad, (((0,), (0,)), ((), ())), preferred_element_type=jnp.float32)
    scaled = (squared * mixing).astype(jnp.bfloat16)
    lower_grad = lax.dot_general(scaled, rows_grad, (((0,), (0,)), ((), ())), preferred_element_type=jnp.float32)
    return input_grad, mix_grad, upper_grad.astype(jnp.bfloat16), lower_grad.astype(jnp.bfloat16)


def reference(latent, grad_out, expert_ids, combine, w_up, w_down):
    group_count = OWNERS // 2
    upper_all = w_up.reshape(group_count, 2, EXP_DEV, LATENT, FH).transpose(0, 2, 3, 1, 4).reshape(EXPERTS, LATENT, HIDDEN_SIZE)
    lower_all = w_down.reshape(group_count, 2, EXP_DEV, FH, LATENT).transpose(0, 2, 1, 3, 4).reshape(EXPERTS, HIDDEN_SIZE, LATENT)
    ranks = block_ranks(expert_ids.reshape(OWNERS, TOK_DEV * TOPK), EXPERTS).reshape(-1).astype(jnp.int32)
    flat_ids = expert_ids.reshape(-1).astype(jnp.int32)
    picks = jnp.arange(TOKENS * TOPK, dtype=jnp.int32)
    source = picks // (TOK_DEV * TOPK)
    table = jnp.full((EXPERTS, OWNERS * CAP), -1, jnp.int32).at[flat_ids, source * CAP + ranks].set(picks)
    mix_flat = combine.reshape(-1)

    def step(carry, inputs):
        lat_acc, mix_acc = carry
        slots, upper, lower = inputs
        valid = slots >= 0
        safe = jnp.where(valid, slots, 0)
        token_rows = safe // TOPK
        rows_in = jnp.where(valid[:, None], latent[token_rows], jnp.zeros((), latent.dtype))
        rows_grad = jnp.where(valid[:, None], grad_out[token_rows], jnp.zeros((), grad_out.dtype))
        rows_mix = jnp.where(valid, mix_flat[safe], jnp.zeros((), combine.dtype))
        input_grad, mix_grad, upper_grad, lower_grad = expert_backward(rows_in, rows_grad, rows_mix, upper, lower)
        lat_acc = lat_acc.at[token_rows].add(jnp.where(valid[:, None], input_grad, jnp.zeros((), jnp.float32)))
        mix_acc = mix_acc.at[safe].add(jnp.where(valid, mix_grad, jnp.zeros((), jnp.float32)))
        return (lat_acc, mix_acc), (upper_grad, lower_grad)

    start = (jnp.zeros((TOKENS, LATENT), jnp.float32), jnp.zeros((TOKENS * TOPK,), jnp.float32))
    (lat_total, mix_total), (upper_grads, lower_grads) = lax.scan(step, start, (table, upper_all, lower_all))
    d_up = upper_grads.reshape(group_count, EXP_DEV, LATENT, 2, FH).transpose(0, 3, 1, 2, 4).reshape(OWNERS, EXP_DEV, LATENT, FH)
    d_down = lower_grads.reshape(group_count, EXP_DEV, 2, FH, LATENT).transpose(0, 2, 1, 3, 4).reshape(OWNERS, EXP_DEV, FH, LATENT)
    return lat_total.astype(jnp.bfloat16), mix_total.reshape(TOKENS, TOPK), d_up, d_down
```

```python
import functools

import jax
import jax.numpy as jnp
from jax import lax
from jax.experimental import pallas as pl
from jax.experimental.pallas import tpu as pltpu
from jax.sharding import PartitionSpec as P

F32 = jnp.float32
BF16 = jnp.bfloat16
CAP = 6
SUB = 8
NN = (((1,), (0,)), ((), ()))
NT = (((1,), (1,)), ((), ()))
TN = (((0,), (0,)), ((), ()))


def dot(a, b, dims=NN):
    return lax.dot_general(a, b, dims, preferred_element_type=F32)


def iota(shape, dim):
    return lax.broadcasted_iota(jnp.int32, shape, dim)


def ones_where(mask):
    return jnp.where(mask, 1.0, 0.0)


def pick_codes(ids_ref, mix_ref, experts):
    tokens = ids_ref.shape[1]
    e_at = iota((experts, tokens), 0)
    hit = jnp.zeros((experts, tokens), F32)
    mix = jnp.zeros((experts, tokens), F32)
    for k in range(ids_ref.shape[0]):
        named = ids_ref[k : k + 1, :] == e_at
        hit = hit + ones_where(named)
        mix = mix + jnp.where(named, mix_ref[k : k + 1, :].astype(F32), 0.0)
    earlier = ones_where(iota((tokens, tokens), 0) < iota((tokens, tokens), 1)).astype(BF16)
    code = hit * (dot(hit.astype(BF16), earlier) + 1.0)
    return code, mix


def pack_kernel(j, ids_ref, mix_ref, lat_ref, grad_ref, out_ref, code_s, mix_s):
    step = pl.program_id(0)
    experts, tokens = code_s.shape
    rows = out_ref.shape[0]

    @pl.when(step == 0)
    def _():
        code, mix = pick_codes(ids_ref, mix_ref, experts)
        code_s[...] = code.astype(BF16)
        mix_s[...] = mix.astype(BF16)

    at = iota((rows, experts), 0) + step * rows
    spread = ones_where(iota((rows, experts), 1) == 2 * (at >> 4) + j).astype(BF16)
    code = dot(spread, code_s[...]).astype(jnp.int32)
    mix = dot(spread, mix_s[...])
    s = iota((rows, tokens), 0) & 7
    lat_hit = ones_where((s < 6) & (code == s + 1))
    grad_a = jnp.where((s >= 6) & (code == s - 5), mix, 0.0)
    grad_lo = jnp.where((s < 4) & (code == s + 3), mix, 0.0)
    grad_hi = jnp.where((s >= 4) & (code == s - 1), mix, 0.0)
    half = lat_ref.shape[1] // 2
    first = jnp.concatenate([lat_hit, grad_a], axis=1).astype(BF16)
    source = jnp.concatenate([lat_ref[...], grad_ref[...]], axis=0)
    out_ref[:, : 2 * half] = dot(first, source).astype(BF16)
    second = jnp.concatenate([grad_lo, grad_hi], axis=1).astype(BF16)
    folded = jnp.concatenate([grad_ref[:, :half], grad_ref[:, half:]], axis=0)
    out_ref[:, 2 * half :] = dot(second, folded).astype(BF16)


def pack(j, ids, mix, lat, grad, experts, owners):
    tokens, width = lat.shape
    rows = owners * SUB
    steps = 4
    whole = lambda a: pl.BlockSpec(a.shape, lambda i: (0, 0))
    return pl.pallas_call(
        functools.partial(pack_kernel, j),
        grid=(steps,),
        in_specs=[whole(ids), whole(mix), whole(lat), whole(grad)],
        out_specs=pl.BlockSpec((rows // steps, 3 * width // 2), lambda i: (i, 0)),
        out_shape=jax.ShapeDtypeStruct((rows, 3 * width // 2), BF16),
        scratch_shapes=[pltpu.VMEM((experts, tokens), BF16), pltpu.VMEM((experts, tokens), BF16)],
        compiler_params=pltpu.CompilerParams(vmem_limit_bytes=24 << 20),
        cost_estimate=pl.CostEstimate(flops=2 * rows * 256 * width * 3 // 2, bytes_accessed=3 * rows * width, transcendentals=0),
        name="pack",
    )(ids, mix, lat, grad)


GROUP = 256
PICKS = GROUP // SUB * CAP


def place(shape, row_dim, rank_of_s, ok):
    other = 1 - row_dim
    pick, row = iota(shape, row_dim), iota(shape, other)
    s = row & 7
    return ones_where((pick == (row >> 3) * CAP + rank_of_s(s)) & ok(s)).astype(BF16)


def expert_kernel(recv_ref, up_ref, down_ref, x_ref, g_ref, hg_ref, sq_ref, back_ref, acc):
    step = pl.program_id(0)
    last = pl.num_programs(0) - 1
    half = x_ref.shape[1] // 2
    groups = recv_ref.shape[0] // GROUP

    @pl.when(step == 0)
    def _():
        shape = (PICKS, GROUP)
        first = jnp.concatenate(
            [
                place(shape, 0, lambda s: s, lambda s: s < 6),
                place(shape, 0, lambda s: s - 6, lambda s: s >= 6),
            ],
            axis=0,
        )
        second = jnp.concatenate(
            [
                place(shape, 0, lambda s: s + 2, lambda s: s < 4),
                place(shape, 0, lambda s: s - 2, lambda s: s >= 4),
            ],
            axis=0,
        )

        def unfold(g, carry):
            raw = pl.ds(pl.multiple_of(g * GROUP, GROUP), GROUP)
            out = pl.ds(pl.multiple_of(g * PICKS, PICKS), PICKS)
            a = dot(first, recv_ref[raw, : 2 * half])
            x_ref[out, :] = a[:PICKS].astype(BF16)
            b = dot(second, recv_ref[raw, 2 * half :])
            g_ref[out, :half] = (a[PICKS:, :half] + b[:PICKS]).astype(BF16)
            g_ref[out, half:] = (a[PICKS:, half:] + b[PICKS:]).astype(BF16)
            return carry

        lax.fori_loop(0, groups, unfold, 0)

    up = up_ref[0, 0]
    pre = dot(up, x_ref[...], NT)
    pulled = dot(down_ref[0, 0], g_ref[...], NT)
    act = jnp.maximum(pre, 0.0)
    sq_ref[...] = (act * act).astype(BF16)
    hg = (2.0 * act * pulled).astype(BF16)
    hg_ref[...] = hg
    part = dot(hg, up, TN)

    @pl.when(step == 0)
    def _():
        acc[...] = part

    @pl.when(step > 0)
    def _():
        acc[...] += part

    @pl.when(step == last)
    def _():
        quarter = half // 2
        shape = (GROUP, PICKS)
        main = place(shape, 1, lambda s: s, lambda s: s < 6)
        rest = [place(shape, 1, lambda s, b=b: s - 6 + 2 * b, lambda s: s >= 6) for b in range(3)]

        def fold(g, carry):
            raw = pl.ds(pl.multiple_of(g * GROUP, GROUP), GROUP)
            src = pl.ds(pl.multiple_of(g * PICKS, PICKS), PICKS)
            y = acc[src, :].astype(BF16)
            tail = y[:, 3 * quarter :]
            for b in range(3):
                cols = slice(b * quarter, (b + 1) * quarter)
                back_ref[raw, cols] = (dot(main, y[:, cols]) + dot(rest[b], tail)).astype(BF16)
            return carry

        lax.fori_loop(0, groups, fold, 0)


def expert_rows(j, recv, up, down, blocks=3):
    rows = recv.shape[0]
    hidden, width = up.shape[2:]
    picks = rows // SUB * CAP
    hb = hidden // blocks
    weight = pl.BlockSpec((1, 1, hb, width), lambda i: (0, j, i, 0))
    fixed = lambda shape: pl.BlockSpec(shape, lambda i: (0, 0))
    slab = pl.BlockSpec((hb, picks), lambda i: (i, 0))
    return pl.pallas_call(
        expert_kernel,
        grid=(blocks,),
        in_specs=[fixed(recv.shape), weight, weight],
        out_specs=[fixed((picks, width)), fixed((picks, width)), slab, slab, fixed((rows, 3 * width // 4))],
        out_shape=[
            jax.ShapeDtypeStruct((picks, width), BF16),
            jax.ShapeDtypeStruct((picks, width), BF16),
            jax.ShapeDtypeStruct((hidden, picks), BF16),
            jax.ShapeDtypeStruct((hidden, picks), BF16),
            jax.ShapeDtypeStruct((rows, 3 * width // 4), BF16),
        ],
        scratch_shapes=[pltpu.VMEM((picks, width), F32)],
        compiler_params=pltpu.CompilerParams(vmem_limit_bytes=48 << 20),
        cost_estimate=pl.CostEstimate(
            flops=6 * picks * hidden * width, bytes_accessed=4 * hidden * width + 4 * hidden * picks + 10 * picks * width, transcendentals=0
        ),
        name="expert_rows",
    )(recv, up, down)


def weights_kernel(hg_ref, sq_ref, x_ref, g_ref, up_ref, down_ref):
    up_ref[...] = dot(hg_ref[...], x_ref[...]).astype(BF16)
    down_ref[...] = dot(sq_ref[...], g_ref[...]).astype(BF16)


def weight_grads(hg, sq, x, g, blocks=3):
    hidden, picks = hg.shape
    width = x.shape[1]
    hb = hidden // blocks
    fixed = lambda shape: pl.BlockSpec(shape, lambda i: (0, 0))
    slab = pl.BlockSpec((hb, picks), lambda i: (i, 0))
    out = pl.BlockSpec((hb, width), lambda i: (i, 0))
    return pl.pallas_call(
        weights_kernel,
        grid=(blocks,),
        in_specs=[slab, slab, fixed((picks, width)), fixed((picks, width))],
        out_specs=[out, out],
        out_shape=[jax.ShapeDtypeStruct((hidden, width), BF16)] * 2,
        compiler_params=pltpu.CompilerParams(vmem_limit_bytes=32 << 20),
        cost_estimate=pl.CostEstimate(
            flops=4 * picks * hidden * width, bytes_accessed=4 * hidden * picks + 4 * picks * width + 4 * hidden * width, transcendentals=0
        ),
        name="weight_grads",
    )(hg, sq, x, g)


def combine_kernel(experts, ids_ref, mix_ref, lat_ref, back0_ref, back1_ref, lat_out, mix_out):
    picks, tokens = ids_ref.shape
    rows = back0_ref.shape[0]
    quarter = lat_ref.shape[1] // 4
    code, _ = pick_codes(ids_ref, mix_ref, experts)
    code = code.astype(BF16)
    s = iota((tokens, rows), 1) & 7
    total = jnp.zeros((tokens, 3 * quarter), F32)
    total_tail = jnp.zeros((tokens, quarter), F32)
    gained = jnp.zeros((experts, tokens), F32)
    for j, back_ref in enumerate((back0_ref, back1_ref)):
        spread = ones_where(iota((experts, rows), 0) == 2 * (iota((experts, rows), 1) >> 4) + j).astype(BF16)
        here = dot(code, spread, TN).astype(jnp.int32)
        main = ones_where((s < 6) & (here == s + 1))
        back = back_ref[...]
        total = total + dot(main.astype(BF16), back)
        dots = main * dot(lat_ref[:, : 3 * quarter], back, NT)
        for b in range(3):
            rest = ones_where((s >= 6) & (here == s - 5 + 2 * b))
            part = back[:, b * quarter : (b + 1) * quarter]
            total_tail = total_tail + dot(rest.astype(BF16), part)
            dots = dots + rest * dot(lat_ref[:, 3 * quarter :], part, NT)
        high = dots.astype(BF16)
        low = (dots - high.astype(F32)).astype(BF16)
        gained = gained + dot(spread, high, NT) + dot(spread, low, NT)
    lat_out[:, : 3 * quarter] = total.astype(BF16)
    lat_out[:, 3 * quarter :] = total_tail.astype(BF16)
    e_at = iota((experts, tokens), 0)
    for k in range(picks):
        dots = jnp.sum(jnp.where(ids_ref[k : k + 1, :] == e_at, gained, 0.0), axis=0, keepdims=True)
        mix_out[k : k + 1, :] = dots / (2.0 * mix_ref[k : k + 1, :].astype(F32))


def combine_back(ids, mix, lat, back0, back1, experts):
    picks, tokens = ids.shape
    return pl.pallas_call(
        functools.partial(combine_kernel, experts),
        out_shape=[jax.ShapeDtypeStruct(lat.shape, BF16), jax.ShapeDtypeStruct((picks, tokens), F32)],
        compiler_params=pltpu.CompilerParams(vmem_limit_bytes=32 << 20),
        name="combine_back",
    )(ids, mix, lat, back0, back1)


AXES = ("node", "local")


def exchange(rows, owners):
    shape = rows.shape
    moved = lax.all_to_all(rows.reshape(owners, SUB, shape[1]), AXES, split_axis=0, concat_axis=0, tiled=True)
    return moved.reshape(shape)


def on_device(latent, grad_out, expert_ids, combine, w_up, w_down):
    owners = lax.axis_size("node") * lax.axis_size("local")
    exp_local = w_up.shape[1]
    experts = owners // 2 * exp_local
    ids, mix = expert_ids.T, combine.T
    up = jnp.swapaxes(w_up, 2, 3)
    backs, d_up, d_down = [], [], []
    for j in range(exp_local):
        recv = exchange(pack(j, ids, mix, latent, grad_out, experts, owners), owners)
        x, g, hg, sq, back = expert_rows(j, recv, up, w_down)
        backs.append(exchange(back, owners))
        du, dv = weight_grads(hg, sq, x, g)
        d_up.append(du)
        d_down.append(dv)
    lat_grad, mix_grad = combine_back(ids, mix, latent, *backs, experts)
    return (
        lat_grad,
        mix_grad.T,
        jnp.swapaxes(jnp.stack(d_up), 1, 2)[None],
        jnp.stack(d_down)[None],
    )


def solution(mesh):
    in_specs = (
        P(AXES, None),
        P(AXES, None),
        P(AXES, None),
        P(AXES, None),
        P(AXES, None, None, None),
        P(AXES, None, None, None),
    )
    out_specs = (
        P(AXES, None),
        P(AXES, None),
        P(AXES, None, None, None),
        P(AXES, None, None, None),
    )
    return jax.shard_map(
        on_device, mesh=mesh, in_specs=in_specs, out_specs=out_specs, check_vma=False
    )
```

```python
import functools

import jax
import jax.numpy as jnp
from jax import lax
from jax.experimental import pallas as pl
from jax.experimental.pallas import tpu as pltpu
from jax.sharding import PartitionSpec as P

F32 = jnp.float32
BF16 = jnp.bfloat16
CAP = 6
SUB = 8
GROUP = 256
MIB = 1 << 20
NN = (((1,), (0,)), ((), ()))
NT = (((1,), (1,)), ((), ()))
TN = (((0,), (0,)), ((), ()))
AXES = ("node", "local")
IN_HBM = pl.BlockSpec(memory_space=pltpu.HBM)


def dot(a, b, dims=NN):
    return lax.dot_general(a, b, dims, preferred_element_type=F32)


def iota(shape, dim):
    return lax.broadcasted_iota(jnp.int32, shape, dim)


def one_hot(mask):
    return jnp.where(mask, 1.0, 0.0).astype(BF16)


def pick_codes(ids, mix, experts):
    tokens = ids.shape[1]
    e_at = iota((experts, tokens), 0)
    hit = jnp.zeros((experts, tokens), F32)
    weight = jnp.zeros((experts, tokens), F32)
    for k in range(ids.shape[0]):
        named = ids[k : k + 1, :] == e_at
        hit = hit + jnp.where(named, 1.0, 0.0)
        weight = weight + jnp.where(named, mix[k : k + 1, :], 0.0)
    earlier = one_hot(iota((tokens, tokens), 0) < iota((tokens, tokens), 1))
    code = hit * (dot(hit.astype(BF16), earlier) + 1.0)
    return code.astype(BF16), weight.astype(BF16)


def slot_masks(code0, code1, s):
    main = jnp.where(s < CAP, code0 - 1, code1 + (CAP - 1)) == s
    main = main & (jnp.where(s < CAP, code0, code1) > 0)
    return main, (s < 4) & (code1 == s + 3), (s >= 4) & (code1 == s - 1)


def pack_kernel(ids_ref, mix_ref, lat_hbm, grad_hbm, out_ref, code_s, weight_s, both_s, sems):
    step = pl.program_id(0)
    experts, tokens = code_s.shape
    rows, width = out_ref.shape[0], lat_hbm.shape[1]

    @pl.when(step == 0)
    def _():
        one = pltpu.make_async_copy(lat_hbm, both_s.at[pl.ds(0, tokens)], sems.at[0])
        two = pltpu.make_async_copy(grad_hbm, both_s.at[pl.ds(tokens, tokens)], sems.at[1])
        one.start()
        two.start()
        code, weight = pick_codes(ids_ref[...], mix_ref[...].astype(F32), experts)
        code_s[...] = code
        weight_s[...] = weight
        one.wait()
        two.wait()

    at = (iota((rows, experts), 0) + step * rows) >> 4
    e_at = iota((rows, experts), 1)
    even, odd = one_hot(e_at == 2 * at), one_hot(e_at == 2 * at + 1)
    s = iota((rows, tokens), 0) & 7
    code0 = dot(even, code_s[...]).astype(jnp.int32)
    code1 = dot(odd, code_s[...]).astype(jnp.int32)
    weight0, weight1 = dot(even, weight_s[...]), dot(odd, weight_s[...])
    main, low, high = slot_masks(code0, code1, s)
    out_ref[:, :width] = dot(one_hot(main), both_s[:tokens, :]).astype(BF16)
    mixed = jnp.where(main, jnp.where(s < CAP, weight0, weight1), 0.0).astype(BF16)
    out_ref[:, width : 2 * width] = dot(mixed, both_s[tokens:, :]).astype(BF16)
    rest = jnp.concatenate([jnp.where(low, 1.0, 0.0), jnp.where(high, weight1, 0.0)], axis=1)
    out_ref[:, 2 * width :] = dot(rest.astype(BF16), both_s[...]).astype(BF16)


def pack(ids, mix, lat, grad, experts, owners):
    tokens, width = lat.shape
    rows, steps = owners * SUB, 4
    whole = lambda a: pl.BlockSpec(a.shape, lambda i: (0, 0))
    return pl.pallas_call(
        pack_kernel,
        grid=(steps,),
        in_specs=[whole(ids), whole(mix), IN_HBM, IN_HBM],
        out_specs=pl.BlockSpec((rows // steps, 3 * width), lambda i: (i, 0)),
        out_shape=jax.ShapeDtypeStruct((rows, 3 * width), BF16),
        scratch_shapes=[
            pltpu.VMEM((experts, tokens), BF16),
            pltpu.VMEM((experts, tokens), BF16),
            pltpu.VMEM((2 * tokens, width), BF16),
            pltpu.SemaphoreType.DMA((2,)),
        ],
        compiler_params=pltpu.CompilerParams(vmem_limit_bytes=60 * MIB),
        cost_estimate=pl.CostEstimate(flops=8 * rows * tokens * width, bytes_accessed=6 * rows * width, transcendentals=0),
        name="pack",
    )(ids, mix, lat, grad)


def slot_order(shape, pick_dim, tail):
    pick, row = iota(shape, pick_dim), iota(shape, 1 - pick_dim)
    source, s = row >> 3, row & 7
    if tail:
        half = GROUP // 2
        return one_hot(pick == jnp.where(s < 4, source * 4 + s, half + source * 4 + s - 4))
    first = GROUP // SUB * CAP
    return one_hot(pick == jnp.where(s < CAP, source * CAP + s, first + source * 2 + s - CAP))


def rows_kernel(
    recv_hbm, up_hbm, down_hbm, x_hbm, g_hbm, hg_hbm, sq_hbm, back_hbm,
    recv_s, up_s, down_s, x_s, g_s, hg_s, sq_s, y_s, back_s, recv_sems, sems, back_sems,
):
    exp_local, hidden, width = up_s.shape
    half, quarter = width // 2, GROUP // 2
    groups = recv_s.shape[0] // GROUP
    picks = x_s.shape[1]
    first = GROUP // SUB * CAP
    second = GROUP - first
    square = (GROUP, GROUP)
    kept = ((x_s, x_hbm), (g_s, g_hbm), (hg_s, hg_hbm), (sq_s, sq_hbm))

    def keep(which, j):
        scratch, hbm = kept[which]
        return pltpu.make_async_copy(scratch.at[j], hbm.at[j], sems.at[which, j])

    def load_rows(i):
        raw = pl.ds(pl.multiple_of(i * GROUP, GROUP), GROUP)
        return pltpu.make_async_copy(recv_hbm.at[raw], recv_s.at[raw], recv_sems.at[i])

    def load_up(j):
        return pltpu.make_async_copy(up_hbm.at[0, j], up_s.at[j], sems.at[4, j])

    def load_down(j):
        return pltpu.make_async_copy(down_hbm.at[0, j], down_s.at[j], sems.at[5, j])

    for i in range(groups):
        load_rows(i).start()
    for j in range(exp_local):
        load_up(j).start()
        load_down(j).start()

    take, take_tail = slot_order(square, 0, False), slot_order(square, 0, True)

    def unfold(i, carry):
        load_rows(i).wait()
        raw = pl.ds(pl.multiple_of(i * GROUP, GROUP), GROUP)
        at = pl.multiple_of(i * first, second)
        whole, head, tail = pl.ds(at, first), pl.ds(at, second), pl.ds(at + second, quarter)
        for to, cols in ((x_s, slice(0, width)), (g_s, slice(width, 2 * width))):
            moved = dot(take, recv_s[raw, cols]).astype(BF16)
            to[0, whole, :] = moved[:first]
            to[1, head, :] = moved[first:]
        moved = dot(take_tail, recv_s[raw, 2 * width :]).astype(BF16)
        x_s[1, tail, :] = moved[:quarter]
        g_s[1, tail, :] = moved[quarter:]
        return carry

    lax.fori_loop(0, groups, unfold, 0)
    for j in range(exp_local):
        keep(0, j).start()
        keep(1, j).start()

    block, tile = hidden // 3, 256
    for j in range(exp_local):
        load_up(j).wait()
        load_down(j).wait()

        def forward(i, carry):
            at = pl.ds(pl.multiple_of(i * block, 64), block)
            pre = dot(up_s[j, at, :], x_s[j], NT)
            pulled = dot(down_s[j, at, :], g_s[j], NT)
            act = jnp.maximum(pre, 0.0)
            sq_s[j, at, :] = (act * act).astype(BF16)
            hg_s[j, at, :] = (2.0 * act * pulled).astype(BF16)
            return carry

        lax.fori_loop(0, 3, forward, 0)
        keep(2, j).start()
        keep(3, j).start()
        for c in range(picks // tile):
            cols = slice(c * tile, (c + 1) * tile)
            y_s[j, cols, :] = dot(hg_s[j, :, cols], up_s[j], TN).astype(BF16)

    put, put_tail = slot_order(square, 1, False), slot_order(square, 1, True)

    def copy_out(i):
        raw = pl.ds(pl.multiple_of(i * GROUP, GROUP), GROUP)
        return pltpu.make_async_copy(back_s.at[raw], back_hbm.at[raw], back_sems.at[i])

    def fold(i, carry):
        raw = pl.ds(pl.multiple_of(i * GROUP, GROUP), GROUP)
        at = pl.multiple_of(i * first, second)
        whole, head, tail = pl.ds(at, first), pl.ds(at, second), pl.ds(at + second, quarter)
        main = jnp.concatenate([y_s[0, whole, :], y_s[1, head, :]], axis=0)
        back_s[raw, :width] = dot(put, main).astype(BF16)
        rest = jnp.concatenate([y_s[1, tail, :half], y_s[1, tail, half:]], axis=0)
        back_s[raw, width:] = dot(put_tail, rest).astype(BF16)
        copy_out(i).start()
        return carry

    lax.fori_loop(0, groups, fold, 0)
    for i in range(groups):
        copy_out(i).wait()
    for which in range(4):
        for j in range(exp_local):
            keep(which, j).wait()


def expert_rows(recv, up, down):
    rows = recv.shape[0]
    _, exp_local, hidden, width = up.shape
    picks = rows // SUB * CAP
    kept = [(exp_local, picks, width)] * 2 + [(exp_local, hidden, picks)] * 2
    back = (rows, 3 * width // 2)
    return pl.pallas_call(
        rows_kernel,
        in_specs=[IN_HBM] * 3,
        out_specs=[IN_HBM] * 5,
        out_shape=[pltpu.HBM(shape, BF16) for shape in kept + [back]],
        scratch_shapes=[pltpu.VMEM(shape, BF16) for shape in [recv.shape, up.shape[1:], up.shape[1:]] + kept + [kept[0], back]]
        + [pltpu.SemaphoreType.DMA(n) for n in ((rows // GROUP,), (6, exp_local), (rows // GROUP,))],
        compiler_params=pltpu.CompilerParams(vmem_limit_bytes=56 * MIB),
        cost_estimate=pl.CostEstimate(flops=6 * exp_local * picks * hidden * width, bytes_accessed=32 * MIB, transcendentals=0),
        name="expert_rows",
    )(recv, up, down)


def weights_kernel(experts, ids_ref, mix_ref, hg_ref, sq_ref, x_ref, g_ref, up_ref, down_ref, masks_ref, spread_ref):
    up_ref[0] = dot(hg_ref[0], x_ref[0]).astype(BF16)
    down_ref[0] = dot(sq_ref[0], g_ref[0]).astype(BF16)

    @pl.when((pl.program_id(0) == 0) & (pl.program_id(1) == 0))
    def _():
        tokens, rows = masks_ref.shape[1:]
        code, _ = pick_codes(ids_ref[...], mix_ref[...].astype(F32), experts)
        s = iota((tokens, rows), 1) & 7
        e_at, pair = iota((experts, rows), 0), 2 * (iota((experts, rows), 1) >> 4)
        even, odd = one_hot(e_at == pair), one_hot(e_at == pair + 1)
        code0 = dot(code, even, TN).astype(jnp.int32)
        code1 = dot(code, odd, TN).astype(jnp.int32)
        for i, mask in enumerate(slot_masks(code0, code1, s)):
            masks_ref[i] = one_hot(mask)
        spread_ref[0] = jnp.where((iota((experts, rows), 1) & 7) < CAP, even, odd)
        spread_ref[1] = odd


def weight_grads(ids, mix, hg, sq, x, g, experts, blocks=3):
    exp_local, hidden, picks = hg.shape
    width = x.shape[2]
    tokens, rows = ids.shape[1], picks // CAP * SUB
    hb = hidden // blocks
    whole = lambda a: pl.BlockSpec(a.shape, lambda j, i: (0,) * a.ndim)
    slab = pl.BlockSpec((1, hb, picks), lambda j, i: (j, i, 0))
    per_expert = pl.BlockSpec((1, picks, width), lambda j, i: (j, 0, 0))
    out = pl.BlockSpec((1, hb, width), lambda j, i: (j, i, 0))
    fixed = lambda n, m: pl.BlockSpec((n, m, rows), lambda j, i: (0, 0, 0))
    return pl.pallas_call(
        functools.partial(weights_kernel, experts),
        grid=(exp_local, blocks),
        in_specs=[whole(ids), whole(mix), slab, slab, per_expert, per_expert],
        out_specs=[out, out, fixed(3, tokens), fixed(2, experts)],
        out_shape=[jax.ShapeDtypeStruct((exp_local, hidden, width), BF16)] * 2
        + [pltpu.HBM((3, tokens, rows), BF16), pltpu.HBM((2, experts, rows), BF16)],
        compiler_params=pltpu.CompilerParams(vmem_limit_bytes=60 * MIB),
        cost_estimate=pl.CostEstimate(flops=4 * exp_local * picks * hidden * width, bytes_accessed=32 * MIB, transcendentals=0),
        name="weight_grads",
    )(ids, mix, hg, sq, x, g)


def combine_kernel(ids_ref, mix_ref, lat_ref, masks_ref, spread_ref, back_ref, lat_out, mix_out):
    picks, tokens = ids_ref.shape
    experts = spread_ref.shape[1]
    width = lat_ref.shape[1]
    half = width // 2
    main, low, high = (masks_ref[i] for i in range(3))
    front, tail = back_ref[:, :width], back_ref[:, width:]
    lat_out[:, :half] = (dot(main, front[:, :half]) + dot(low, tail)).astype(BF16)
    lat_out[:, half:] = (dot(main, front[:, half:]) + dot(high, tail)).astype(BF16)
    tail_dots = low.astype(F32) * dot(lat_ref[:, :half], tail, NT) + high.astype(F32) * dot(lat_ref[:, half:], tail, NT)
    gained = jnp.zeros((experts, tokens), F32)
    for i, dots in enumerate((main.astype(F32) * dot(lat_ref[...], front, NT), tail_dots)):
        upper = dots.astype(BF16)
        lower = (dots - upper.astype(F32)).astype(BF16)
        gained = gained + dot(spread_ref[i], upper, NT) + dot(spread_ref[i], lower, NT)
    e_at = iota((experts, tokens), 0)
    for k in range(picks):
        dots = jnp.sum(jnp.where(ids_ref[k : k + 1, :] == e_at, gained, 0.0), axis=0, keepdims=True)
        mix_out[k : k + 1, :] = dots / (2.0 * mix_ref[k : k + 1, :].astype(F32))


def combine_back(ids, mix, lat, masks, spread, back):
    return pl.pallas_call(
        combine_kernel,
        out_shape=[jax.ShapeDtypeStruct(lat.shape, BF16), jax.ShapeDtypeStruct(ids.shape, F32)],
        compiler_params=pltpu.CompilerParams(vmem_limit_bytes=32 * MIB),
        name="combine_back",
    )(ids, mix, lat, masks, spread, back)


def exchange(rows, owners):
    shape = rows.shape
    moved = lax.all_to_all(rows.reshape(owners, SUB, shape[1]), AXES, split_axis=0, concat_axis=0, tiled=True)
    return moved.reshape(shape)


def on_device(latent, grad_out, expert_ids, combine, w_up, w_down):
    owners = lax.axis_size("node") * lax.axis_size("local")
    experts = owners // 2 * w_up.shape[1]
    ids, mix = expert_ids.T, combine.T
    recv = exchange(pack(ids, mix, latent, grad_out, experts, owners), owners)
    x, g, hg, sq, back = expert_rows(recv, jnp.swapaxes(w_up, 2, 3), w_down)
    returned = exchange(back, owners)
    d_up, d_down, masks, spread = weight_grads(ids, mix, hg, sq, x, g, experts)
    lat_grad, mix_grad = combine_back(ids, mix, latent, masks, spread, returned)
    return lat_grad, mix_grad.T, jnp.swapaxes(d_up, 1, 2)[None], d_down[None]


def solution(mesh):
    in_specs = (
        P(AXES, None),
        P(AXES, None),
        P(AXES, None),
        P(AXES, None),
        P(AXES, None, None, None),
        P(AXES, None, None, None),
    )
    out_specs = (
        P(AXES, None),
        P(AXES, None),
        P(AXES, None, None, None),
        P(AXES, None, None, None),
    )
    return jax.shard_map(
        on_device, mesh=mesh, in_specs=in_specs, out_specs=out_specs, check_vma=False
    )
```

```python
import functools

import jax
import jax.numpy as jnp
from jax import lax
from jax.experimental import pallas as pl
from jax.experimental.pallas import tpu as pltpu
from jax.sharding import PartitionSpec as P

F32 = jnp.float32
BF16 = jnp.bfloat16
CAP = 6
SUB = 8
GROUP = 256
MIB = 1 << 20
NN = (((1,), (0,)), ((), ()))
NT = (((1,), (1,)), ((), ()))
TN = (((0,), (0,)), ((), ()))
AXES = ("node", "local")
IN_HBM = pl.BlockSpec(memory_space=pltpu.HBM)
IN_VMEM = pl.BlockSpec(memory_space=pltpu.VMEM)


def dot(a, b, dims=NN):
    return lax.dot_general(a, b, dims, preferred_element_type=F32)


def iota(shape, dim):
    return lax.broadcasted_iota(jnp.int32, shape, dim)


def pinned(a):
    return pltpu.with_memory_space_constraint(a, pltpu.HBM)


def one_hot(mask):
    return jnp.where(mask, 1.0, 0.0).astype(BF16)


def pick_codes(ids, mix, experts):
    tokens = ids.shape[1]
    e_at = iota((experts, tokens), 0)
    hit = jnp.zeros((experts, tokens), F32)
    weight = jnp.zeros((experts, tokens), F32)
    for k in range(ids.shape[0]):
        named = ids[k : k + 1, :] == e_at
        hit = hit + jnp.where(named, 1.0, 0.0)
        weight = weight + jnp.where(named, mix[k : k + 1, :], 0.0)
    earlier = one_hot(iota((tokens, tokens), 0) < iota((tokens, tokens), 1))
    code = hit * (dot(hit.astype(BF16), earlier) + 1.0)
    return code.astype(BF16), weight.astype(BF16)


def slot_masks(code0, code1, s):
    main = jnp.where(s < CAP, code0 - 1, code1 + (CAP - 1)) == s
    main = main & (jnp.where(s < CAP, code0, code1) > 0)
    return main, (s < 4) & (code1 == s + 3), (s >= 4) & (code1 == s - 1)


def pack_kernel(ids_ref, mix_ref, lat_hbm, grad_hbm, out_ref, code_s, weight_s, both_s, sems):
    step = pl.program_id(0)
    experts, tokens = code_s.shape
    rows, width = out_ref.shape[0], lat_hbm.shape[1]

    @pl.when(step == 0)
    def _():
        one = pltpu.make_async_copy(lat_hbm, both_s.at[pl.ds(0, tokens)], sems.at[0])
        two = pltpu.make_async_copy(grad_hbm, both_s.at[pl.ds(tokens, tokens)], sems.at[1])
        one.start()
        two.start()
        code, weight = pick_codes(ids_ref[...], mix_ref[...].astype(F32), experts)
        code_s[...] = code
        weight_s[...] = weight
        one.wait()
        two.wait()

    half = rows // 2
    at = (iota((half, experts), 0) + step * half) >> 3
    e_at = iota((half, experts), 1)
    even, odd = one_hot(e_at == 2 * at), one_hot(e_at == 2 * at + 1)
    s = iota((half, tokens), 0) & 7
    code0 = dot(even, code_s[...]).astype(jnp.int32)
    code1 = dot(odd, code_s[...]).astype(jnp.int32)
    weight0, weight1 = dot(even, weight_s[...]), dot(odd, weight_s[...])
    main, low, high = slot_masks(code0, code1, s)

    def twice(a):
        a = a.reshape(half // SUB, 1, SUB, width)
        return jnp.broadcast_to(a, (half // SUB, 2, SUB, width)).reshape(rows, width).astype(BF16)

    out_ref[:, :width] = twice(dot(one_hot(main), both_s[:tokens, :]))
    mixed = jnp.where(main, jnp.where(s < CAP, weight0, weight1), 0.0).astype(BF16)
    out_ref[:, width : 2 * width] = twice(dot(mixed, both_s[tokens:, :]))
    rest = jnp.concatenate([jnp.where(low, 1.0, 0.0), jnp.where(high, weight1, 0.0)], axis=1)
    out_ref[:, 2 * width :] = twice(dot(rest.astype(BF16), both_s[...]))


def pack(ids, mix, lat, grad, experts, owners):
    tokens, width = lat.shape
    rows, steps = owners * SUB, 2
    whole = lambda a: pl.BlockSpec(a.shape, lambda i: (0, 0))
    return pl.pallas_call(
        pack_kernel,
        grid=(steps,),
        in_specs=[whole(ids), whole(mix), IN_HBM, IN_HBM],
        out_specs=pl.BlockSpec((rows // steps, 3 * width), lambda i: (i, 0)),
        out_shape=jax.ShapeDtypeStruct((rows, 3 * width), BF16),
        scratch_shapes=[
            pltpu.VMEM((experts, tokens), BF16),
            pltpu.VMEM((experts, tokens), BF16),
            pltpu.VMEM((2 * tokens, width), BF16),
            pltpu.SemaphoreType.DMA((2,)),
        ],
        compiler_params=pltpu.CompilerParams(vmem_limit_bytes=60 * MIB),
        cost_estimate=pl.CostEstimate(flops=8 * rows * tokens * width, bytes_accessed=6 * rows * width, transcendentals=0),
        name="pack",
    )(ids, mix, lat, grad)


def slot_order(shape, pick_dim, tail):
    pick, row = iota(shape, pick_dim), iota(shape, 1 - pick_dim)
    source, s = row >> 3, row & 7
    if tail:
        half = GROUP // 2
        return one_hot(pick == jnp.where(s < 4, source * 4 + s, half + source * 4 + s - 4))
    first = GROUP // SUB * CAP
    return one_hot(pick == jnp.where(s < CAP, source * CAP + s, first + source * 2 + s - CAP))


def rows_kernel(
    recv_ref, up_ref, down_ref, x_hbm, g_hbm, hg_hbm, sq_hbm, back_hbm,
    x_s, g_s, hg_s, sq_s, y_s, back_s, sems, back_sems,
):
    exp_local, hidden, width = up_ref.shape[1:]
    half, quarter = width // 2, GROUP // 2
    groups = recv_ref.shape[0] // GROUP
    picks = x_s.shape[1]
    first = GROUP // SUB * CAP
    second = GROUP - first
    square = (GROUP, GROUP)
    kept = ((x_s, x_hbm), (g_s, g_hbm), (hg_s, hg_hbm), (sq_s, sq_hbm))

    def keep(which, j):
        scratch, hbm = kept[which]
        return pltpu.make_async_copy(scratch.at[j], hbm.at[j], sems.at[which, j])

    take, take_tail = slot_order(square, 0, False), slot_order(square, 0, True)

    def unfold(i, carry):
        raw = pl.ds(pl.multiple_of(i * GROUP, GROUP), GROUP)
        at = pl.multiple_of(i * first, second)
        whole, head, tail = pl.ds(at, first), pl.ds(at, second), pl.ds(at + second, quarter)
        for to, cols in ((x_s, slice(0, width)), (g_s, slice(width, 2 * width))):
            moved = dot(take, recv_ref[raw, cols]).astype(BF16)
            to[0, whole, :] = moved[:first]
            to[1, head, :] = moved[first:]
        moved = dot(take_tail, recv_ref[raw, 2 * width :]).astype(BF16)
        x_s[1, tail, :] = moved[:quarter]
        g_s[1, tail, :] = moved[quarter:]
        return carry

    lax.fori_loop(0, groups, unfold, 0)
    for j in range(exp_local):
        keep(0, j).start()
        keep(1, j).start()

    blocks = 1
    block = hidden // blocks
    for j in range(exp_local):

        def forward(i, carry):
            at = pl.ds(pl.multiple_of(i * block, 64), block)
            pre = dot(up_ref[0, j, at, :], x_s[j], NT)
            pulled = dot(down_ref[0, j, at, :], g_s[j], NT)
            act = jnp.maximum(pre, 0.0)
            sq_s[j, at, :] = (act * act).astype(BF16)
            hg_s[j, at, :] = (2.0 * act * pulled).astype(BF16)
            return carry

        lax.fori_loop(0, blocks, forward, 0)
        keep(2, j).start()
        keep(3, j).start()
        y_s[j] = dot(hg_s[j], up_ref[0, j], TN).astype(BF16)

    put, put_tail = slot_order(square, 1, False), slot_order(square, 1, True)

    def copy_out(i):
        raw = pl.ds(pl.multiple_of(i * GROUP, GROUP), GROUP)
        return pltpu.make_async_copy(back_s.at[raw], back_hbm.at[raw], back_sems.at[i])

    def fold(i, carry):
        raw = pl.ds(pl.multiple_of(i * GROUP, GROUP), GROUP)
        at = pl.multiple_of(i * first, second)
        whole, head, tail = pl.ds(at, first), pl.ds(at, second), pl.ds(at + second, quarter)
        main = jnp.concatenate([y_s[0, whole, :], y_s[1, head, :]], axis=0)
        back_s[raw, :width] = dot(put, main).astype(BF16)
        rest = jnp.concatenate([y_s[1, tail, :half], y_s[1, tail, half:]], axis=0)
        back_s[raw, width:] = dot(put_tail, rest).astype(BF16)
        copy_out(i).start()
        return carry

    lax.fori_loop(0, groups, fold, 0)
    for i in range(groups):
        copy_out(i).wait()
    for which in range(4):
        for j in range(exp_local):
            keep(which, j).wait()


def expert_rows(recv, up, down):
    rows = recv.shape[0]
    _, exp_local, hidden, width = up.shape
    picks = rows // SUB * CAP
    kept = [(exp_local, picks, width)] * 2 + [(exp_local, hidden, picks)] * 2
    back = (rows, 3 * width // 2)
    return pl.pallas_call(
        rows_kernel,
        in_specs=[IN_VMEM] * 3,
        out_specs=[IN_HBM] * 5,
        out_shape=[pltpu.HBM(shape, BF16) for shape in kept + [back]],
        scratch_shapes=[pltpu.VMEM(shape, BF16) for shape in kept + [kept[0], back]]
        + [pltpu.SemaphoreType.DMA(n) for n in ((4, exp_local), (rows // GROUP,))],
        compiler_params=pltpu.CompilerParams(vmem_limit_bytes=36 * MIB),
        cost_estimate=pl.CostEstimate(flops=6 * exp_local * picks * hidden * width, bytes_accessed=32 * MIB, transcendentals=0),
        name="expert_rows",
    )(recv, up, down)


def weights_kernel(experts, ids_ref, mix_ref, hg_ref, sq_ref, x_ref, g_ref, up_ref, down_ref, masks_ref, spread_ref):
    up_ref[0] = dot(hg_ref[0], x_ref[0]).astype(BF16)
    down_ref[0] = dot(sq_ref[0], g_ref[0]).astype(BF16)

    @pl.when((pl.program_id(0) == 0) & (pl.program_id(1) == 0))
    def _():
        tokens, rows = masks_ref.shape[1:]
        code, _ = pick_codes(ids_ref[...], mix_ref[...].astype(F32), experts)
        s = iota((tokens, rows), 1) & 7
        e_at, pair = iota((experts, rows), 0), 2 * (iota((experts, rows), 1) >> 4)
        even, odd = one_hot(e_at == pair), one_hot(e_at == pair + 1)
        code0 = dot(code, even, TN).astype(jnp.int32)
        code1 = dot(code, odd, TN).astype(jnp.int32)
        for i, mask in enumerate(slot_masks(code0, code1, s)):
            masks_ref[i] = one_hot(mask)
        spread_ref[0] = jnp.where((iota((experts, rows), 1) & 7) < CAP, even, odd)
        spread_ref[1] = odd


def weight_grads(ids, mix, hg, sq, x, g, experts, blocks=3):
    exp_local, hidden, picks = hg.shape
    width = x.shape[2]
    tokens, rows = ids.shape[1], picks // CAP * SUB
    hb = hidden // blocks
    whole = lambda a: pl.BlockSpec(a.shape, lambda j, i: (0,) * a.ndim)
    slab = pl.BlockSpec((1, hb, picks), lambda j, i: (j, i, 0))
    per_expert = pl.BlockSpec((1, picks, width), lambda j, i: (j, 0, 0))
    out = pl.BlockSpec((1, hb, width), lambda j, i: (j, i, 0))
    fixed = lambda n, m: pl.BlockSpec((n, m, rows), lambda j, i: (0, 0, 0))
    return pl.pallas_call(
        functools.partial(weights_kernel, experts),
        grid=(exp_local, blocks),
        in_specs=[whole(ids), whole(mix), slab, slab, per_expert, per_expert],
        out_specs=[out, out, fixed(3, tokens), fixed(2, experts)],
        out_shape=[jax.ShapeDtypeStruct((exp_local, hidden, width), BF16)] * 2
        + [pltpu.HBM((3, tokens, rows), BF16), pltpu.HBM((2, experts, rows), BF16)],
        compiler_params=pltpu.CompilerParams(vmem_limit_bytes=60 * MIB),
        cost_estimate=pl.CostEstimate(flops=4 * exp_local * picks * hidden * width, bytes_accessed=32 * MIB, transcendentals=0),
        name="weight_grads",
    )(ids, mix, hg, sq, x, g)


def combine_kernel(ids_ref, mix_ref, lat_ref, masks_ref, spread_ref, back_ref, lat_out, mix_out):
    picks, tokens = ids_ref.shape
    experts = spread_ref.shape[1]
    width = lat_ref.shape[1]
    half = width // 2
    main, low, high = (masks_ref[i] for i in range(3))
    front, tail = back_ref[:, :width], back_ref[:, width:]
    lat_out[:, :half] = (dot(main, front[:, :half]) + dot(low, tail)).astype(BF16)
    lat_out[:, half:] = (dot(main, front[:, half:]) + dot(high, tail)).astype(BF16)
    tail_dots = low.astype(F32) * dot(lat_ref[:, :half], tail, NT) + high.astype(F32) * dot(lat_ref[:, half:], tail, NT)
    gained = jnp.zeros((experts, tokens), F32)
    for i, dots in enumerate((main.astype(F32) * dot(lat_ref[...], front, NT), tail_dots)):
        upper = dots.astype(BF16)
        lower = (dots - upper.astype(F32)).astype(BF16)
        gained = gained + dot(spread_ref[i], upper, NT) + dot(spread_ref[i], lower, NT)
    e_at = iota((experts, tokens), 0)
    for k in range(picks):
        dots = jnp.sum(jnp.where(ids_ref[k : k + 1, :] == e_at, gained, 0.0), axis=0, keepdims=True)
        mix_out[k : k + 1, :] = dots / (2.0 * mix_ref[k : k + 1, :].astype(F32))


def combine_back(ids, mix, lat, masks, spread, back):
    return pl.pallas_call(
        combine_kernel,
        out_shape=[jax.ShapeDtypeStruct(lat.shape, BF16), jax.ShapeDtypeStruct(ids.shape, F32)],
        compiler_params=pltpu.CompilerParams(vmem_limit_bytes=32 * MIB),
        name="combine_back",
    )(ids, mix, lat, pinned(masks), pinned(spread), back)


def exchange(rows, owners):
    shape = rows.shape
    moved = lax.all_to_all(rows.reshape(owners, SUB, shape[1]), AXES, split_axis=0, concat_axis=0, tiled=True)
    return moved.reshape(shape)


def on_device(latent, grad_out, expert_ids, combine, w_up, w_down):
    owners = lax.axis_size("node") * lax.axis_size("local")
    experts = owners // 2 * w_up.shape[1]
    ids, mix = expert_ids.T, combine.T
    recv = exchange(pack(ids, mix, latent, grad_out, experts, owners), owners)
    x, g, hg, sq, back = expert_rows(recv, jnp.swapaxes(w_up, 2, 3), w_down)
    returned = exchange(back, owners)
    d_up, d_down, masks, spread = weight_grads(ids, mix, hg, sq, x, g, experts)
    lat_grad, mix_grad = combine_back(ids, mix, latent, masks, spread, returned)
    return lat_grad, mix_grad.T, jnp.swapaxes(d_up, 1, 2)[None], d_down[None]


def solution(mesh):
    in_specs = (
        P(AXES, None),
        P(AXES, None),
        P(AXES, None),
        P(AXES, None),
        P(AXES, None, None, None),
        P(AXES, None, None, None),
    )
    out_specs = (
        P(AXES, None),
        P(AXES, None),
        P(AXES, None, None, None),
        P(AXES, None, None, None),
    )
    return jax.shard_map(
        on_device, mesh=mesh, in_specs=in_specs, out_specs=out_specs, check_vma=False
    )
```

```python
import functools

import jax
import jax.numpy as jnp
from jax import lax
from jax.experimental import pallas as pl
from jax.experimental.pallas import tpu as pltpu
from jax.sharding import PartitionSpec as P

F32 = jnp.float32
BF16 = jnp.bfloat16
CAP = 6
SUB = 8
GROUP = 256
MIB = 1 << 20
NN = (((1,), (0,)), ((), ()))
NT = (((1,), (1,)), ((), ()))
TN = (((0,), (0,)), ((), ()))
AXES = ("node", "local")
IN_HBM = pl.BlockSpec(memory_space=pltpu.HBM)
IN_VMEM = pl.BlockSpec(memory_space=pltpu.VMEM)


def dot(a, b, dims=NN):
    return lax.dot_general(a, b, dims, preferred_element_type=F32)


def iota(shape, dim):
    return lax.broadcasted_iota(jnp.int32, shape, dim)


def pinned(a):
    return pltpu.with_memory_space_constraint(a, pltpu.HBM)


def one_hot(mask):
    return jnp.where(mask, 1.0, 0.0).astype(BF16)


def pick_codes(ids, mix, experts):
    tokens = ids.shape[1]
    e_at = iota((experts, tokens), 0)
    hit = jnp.zeros((experts, tokens), F32)
    weight = jnp.zeros((experts, tokens), F32)
    for k in range(ids.shape[0]):
        named = ids[k : k + 1, :] == e_at
        hit = hit + jnp.where(named, 1.0, 0.0)
        weight = weight + jnp.where(named, mix[k : k + 1, :], 0.0)
    earlier = one_hot(iota((tokens, tokens), 0) < iota((tokens, tokens), 1))
    code = hit * (dot(hit.astype(BF16), earlier) + 1.0)
    return code.astype(BF16), weight.astype(BF16)


def slot_masks(code0, code1, s):
    main = jnp.where(s < CAP, code0 - 1, code1 + (CAP - 1)) == s
    main = main & (jnp.where(s < CAP, code0, code1) > 0)
    return main, (s < 4) & (code1 == s + 3), (s >= 4) & (code1 == s - 1)


def pack_kernel(ids_hbm, mix_hbm, lat_hbm, grad_hbm, out_ref, ids_s, mix_s, both_s, sems):
    tokens, width = lat_hbm.shape
    rows, experts = out_ref.shape[0], out_ref.shape[0] // SUB
    half, part = rows // 2, rows // 4
    loads = [
        pltpu.make_async_copy(hbm, to, sems.at[i])
        for i, (hbm, to) in enumerate(
            (
                (ids_hbm, ids_s),
                (mix_hbm, mix_s),
                (lat_hbm, both_s.at[pl.ds(0, tokens)]),
                (grad_hbm, both_s.at[pl.ds(tokens, tokens)]),
            )
        )
    ]
    for load in loads:
        load.start()
    at = iota((half, experts), 0) >> 3
    e_at = iota((half, experts), 1)
    even, odd = one_hot(e_at == 2 * at), one_hot(e_at == 2 * at + 1)
    s = iota((half, tokens), 0) & 7
    loads[0].wait()
    loads[1].wait()
    code, weight = pick_codes(ids_s[...], mix_s[...].astype(F32), experts)
    code0, code1 = dot(even, code).astype(jnp.int32), dot(odd, code).astype(jnp.int32)
    weight0, weight1 = dot(even, weight), dot(odd, weight)
    main, low, high = slot_masks(code0, code1, s)
    plain = one_hot(main)
    mixed = jnp.where(main, jnp.where(s < CAP, weight0, weight1), 0.0).astype(BF16)
    rest = jnp.concatenate([jnp.where(low, 1.0, 0.0), jnp.where(high, weight1, 0.0)], axis=1).astype(BF16)
    loads[2].wait()
    loads[3].wait()

    def twice(a):
        a = a.reshape(part // SUB, 1, SUB, width)
        return jnp.broadcast_to(a, (part // SUB, 2, SUB, width)).reshape(2 * part, width).astype(BF16)

    for i in range(2):
        here, to = slice(i * part, (i + 1) * part), slice(i * 2 * part, (i + 1) * 2 * part)
        out_ref[to, :width] = twice(dot(plain[here], both_s[:tokens, :]))
        out_ref[to, width : 2 * width] = twice(dot(mixed[here], both_s[tokens:, :]))
        out_ref[to, 2 * width :] = twice(dot(rest[here], both_s[...]))


def pack(ids, mix, lat, grad, owners):
    tokens, width = lat.shape
    rows = owners * SUB
    return pl.pallas_call(
        pack_kernel,
        in_specs=[IN_HBM] * 4,
        out_specs=IN_VMEM,
        out_shape=jax.ShapeDtypeStruct((rows, 3 * width), BF16),
        scratch_shapes=[
            pltpu.VMEM(ids.shape, jnp.int32),
            pltpu.VMEM(mix.shape, BF16),
            pltpu.VMEM((2 * tokens, width), BF16),
            pltpu.SemaphoreType.DMA((4,)),
        ],
        compiler_params=pltpu.CompilerParams(vmem_limit_bytes=24 * MIB),
        cost_estimate=pl.CostEstimate(flops=8 * rows * tokens * width, bytes_accessed=6 * rows * width, transcendentals=0),
        name="pack",
    )(pinned(ids), pinned(mix), pinned(lat), pinned(grad))


def slot_order(shape, pick_dim, tail):
    pick, row = iota(shape, pick_dim), iota(shape, 1 - pick_dim)
    source, s = row >> 3, row & 7
    if tail:
        half = GROUP // 2
        return one_hot(pick == jnp.where(s < 4, source * 4 + s, half + source * 4 + s - 4))
    first = GROUP // SUB * CAP
    return one_hot(pick == jnp.where(s < CAP, source * CAP + s, first + source * 2 + s - CAP))


def rows_kernel(
    recv_ref, up_ref, down_ref, x_hbm, g_hbm, hg_hbm, sq_hbm, back_hbm,
    x_s, g_s, hg_s, sq_s, y_s, back_s, sems, back_sems,
):
    exp_local, hidden, width = up_ref.shape[1:]
    half, quarter = width // 2, GROUP // 2
    groups = recv_ref.shape[0] // GROUP
    picks = x_s.shape[1]
    first = GROUP // SUB * CAP
    second = GROUP - first
    square = (GROUP, GROUP)
    kept = ((x_s, x_hbm), (g_s, g_hbm), (hg_s, hg_hbm), (sq_s, sq_hbm))

    def keep(which, j):
        scratch, hbm = kept[which]
        return pltpu.make_async_copy(scratch.at[j], hbm.at[j], sems.at[which, j])

    take, take_tail = slot_order(square, 0, False), slot_order(square, 0, True)

    def unfold(i, carry):
        raw = pl.ds(pl.multiple_of(i * GROUP, GROUP), GROUP)
        at = pl.multiple_of(i * first, second)
        whole, head, tail = pl.ds(at, first), pl.ds(at, second), pl.ds(at + second, quarter)
        for to, cols in ((x_s, slice(0, width)), (g_s, slice(width, 2 * width))):
            moved = dot(take, recv_ref[raw, cols]).astype(BF16)
            to[0, whole, :] = moved[:first]
            to[1, head, :] = moved[first:]
        moved = dot(take_tail, recv_ref[raw, 2 * width :]).astype(BF16)
        x_s[1, tail, :] = moved[:quarter]
        g_s[1, tail, :] = moved[quarter:]
        return carry

    lax.fori_loop(0, groups, unfold, 0)
    for j in range(exp_local):
        keep(0, j).start()
        keep(1, j).start()

    blocks = 1
    block = hidden // blocks
    for j in range(exp_local):

        def forward(i, carry):
            at = pl.ds(pl.multiple_of(i * block, 64), block)
            pre = dot(up_ref[0, j, at, :], x_s[j], NT)
            pulled = dot(down_ref[0, j, at, :], g_s[j], NT)
            act = jnp.maximum(pre, 0.0)
            sq_s[j, at, :] = (act * act).astype(BF16)
            hg_s[j, at, :] = (2.0 * act * pulled).astype(BF16)
            return carry

        lax.fori_loop(0, blocks, forward, 0)
        keep(2, j).start()
        keep(3, j).start()
        y_s[j] = dot(hg_s[j], up_ref[0, j], TN).astype(BF16)

    put, put_tail = slot_order(square, 1, False), slot_order(square, 1, True)

    def copy_out(i):
        raw = pl.ds(pl.multiple_of(i * GROUP, GROUP), GROUP)
        return pltpu.make_async_copy(back_s.at[raw], back_hbm.at[raw], back_sems.at[i])

    def fold(i, carry):
        raw = pl.ds(pl.multiple_of(i * GROUP, GROUP), GROUP)
        at = pl.multiple_of(i * first, second)
        whole, head, tail = pl.ds(at, first), pl.ds(at, second), pl.ds(at + second, quarter)
        main = jnp.concatenate([y_s[0, whole, :], y_s[1, head, :]], axis=0)
        back_s[raw, :width] = dot(put, main).astype(BF16)
        rest = jnp.concatenate([y_s[1, tail, :half], y_s[1, tail, half:]], axis=0)
        back_s[raw, width:] = dot(put_tail, rest).astype(BF16)
        copy_out(i).start()
        return carry

    lax.fori_loop(0, groups, fold, 0)
    for i in range(groups):
        copy_out(i).wait()
    for which in range(4):
        for j in range(exp_local):
            keep(which, j).wait()


def expert_rows(recv, up, down):
    rows = recv.shape[0]
    _, exp_local, hidden, width = up.shape
    picks = rows // SUB * CAP
    kept = [(exp_local, picks, width)] * 2 + [(exp_local, hidden, picks)] * 2
    back = (rows, 3 * width // 2)
    return pl.pallas_call(
        rows_kernel,
        in_specs=[IN_VMEM] * 3,
        out_specs=[IN_HBM] * 5,
        out_shape=[pltpu.HBM(shape, BF16) for shape in kept + [back]],
        scratch_shapes=[pltpu.VMEM(shape, BF16) for shape in kept + [kept[0], back]]
        + [pltpu.SemaphoreType.DMA(n) for n in ((4, exp_local), (rows // GROUP,))],
        compiler_params=pltpu.CompilerParams(vmem_limit_bytes=36 * MIB),
        cost_estimate=pl.CostEstimate(flops=6 * exp_local * picks * hidden * width, bytes_accessed=32 * MIB, transcendentals=0),
        name="expert_rows",
    )(recv, up, down)


def weights_kernel(experts, ids_ref, mix_ref, hg_ref, sq_ref, x_ref, g_ref, up_ref, down_ref, masks_ref, spread_ref):
    up_ref[0] = dot(hg_ref[0], x_ref[0]).astype(BF16)
    down_ref[0] = dot(sq_ref[0], g_ref[0]).astype(BF16)

    @pl.when((pl.program_id(0) == 0) & (pl.program_id(1) == 0))
    def _():
        tokens, rows = masks_ref.shape[1:]
        code, _ = pick_codes(ids_ref[...], mix_ref[...].astype(F32), experts)
        s = iota((tokens, rows), 1) & 7
        e_at, pair = iota((experts, rows), 0), 2 * (iota((experts, rows), 1) >> 4)
        even, odd = one_hot(e_at == pair), one_hot(e_at == pair + 1)
        code0 = dot(code, even, TN).astype(jnp.int32)
        code1 = dot(code, odd, TN).astype(jnp.int32)
        for i, mask in enumerate(slot_masks(code0, code1, s)):
            masks_ref[i] = one_hot(mask)
        spread_ref[0] = jnp.where((iota((experts, rows), 1) & 7) < CAP, even, odd)
        spread_ref[1] = odd


def weight_grads(ids, mix, hg, sq, x, g, experts, blocks=3):
    exp_local, hidden, picks = hg.shape
    width = x.shape[2]
    tokens, rows = ids.shape[1], picks // CAP * SUB
    hb = hidden // blocks
    whole = lambda a: pl.BlockSpec(a.shape, lambda j, i: (0,) * a.ndim)
    slab = pl.BlockSpec((1, hb, picks), lambda j, i: (j, i, 0))
    per_expert = pl.BlockSpec((1, picks, width), lambda j, i: (j, 0, 0))
    out = pl.BlockSpec((1, hb, width), lambda j, i: (j, i, 0))
    fixed = lambda n, m: pl.BlockSpec((n, m, rows), lambda j, i: (0, 0, 0))
    return pl.pallas_call(
        functools.partial(weights_kernel, experts),
        grid=(exp_local, blocks),
        in_specs=[whole(ids), whole(mix), slab, slab, per_expert, per_expert],
        out_specs=[out, out, fixed(3, tokens), fixed(2, experts)],
        out_shape=[jax.ShapeDtypeStruct((exp_local, hidden, width), BF16)] * 2
        + [pltpu.HBM((3, tokens, rows), BF16), pltpu.HBM((2, experts, rows), BF16)],
        compiler_params=pltpu.CompilerParams(vmem_limit_bytes=60 * MIB),
        cost_estimate=pl.CostEstimate(flops=4 * exp_local * picks * hidden * width, bytes_accessed=32 * MIB, transcendentals=0),
        name="weight_grads",
    )(ids, mix, hg, sq, x, g)


def combine_kernel(ids_ref, mix_ref, lat_ref, masks_hbm, spread_hbm, back_ref, lat_out, mix_out, masks_s, spread_s, sems):
    picks, tokens = ids_ref.shape
    experts = spread_s.shape[1]
    width = lat_ref.shape[1]
    half = width // 2
    load_masks = pltpu.make_async_copy(masks_hbm, masks_s, sems.at[0])
    load_spread = pltpu.make_async_copy(spread_hbm, spread_s, sems.at[1])
    load_masks.start()
    load_spread.start()
    front_dots = dot(lat_ref[...], back_ref[:, :width], NT)
    low_dots = dot(lat_ref[:, :half], back_ref[:, width:], NT)
    high_dots = dot(lat_ref[:, half:], back_ref[:, width:], NT)
    load_masks.wait()
    main, low, high = (masks_s[i] for i in range(3))
    tail = back_ref[:, width:]
    lat_out[:, :half] = (dot(main, back_ref[:, :half]) + dot(low, tail)).astype(BF16)
    lat_out[:, half:] = (dot(main, back_ref[:, half:width]) + dot(high, tail)).astype(BF16)
    load_spread.wait()
    gained = jnp.zeros((experts, tokens), F32)
    for i, dots in enumerate((main.astype(F32) * front_dots, low.astype(F32) * low_dots + high.astype(F32) * high_dots)):
        upper = dots.astype(BF16)
        lower = (dots - upper.astype(F32)).astype(BF16)
        gained = gained + dot(spread_s[i], upper, NT) + dot(spread_s[i], lower, NT)
    e_at = iota((experts, tokens), 0)
    for k in range(picks):
        dots = jnp.sum(jnp.where(ids_ref[k : k + 1, :] == e_at, gained, 0.0), axis=0, keepdims=True)
        mix_out[k : k + 1, :] = dots / (2.0 * mix_ref[k : k + 1, :].astype(F32))


def combine_back(ids, mix, lat, masks, spread, back):
    return pl.pallas_call(
        combine_kernel,
        in_specs=[IN_VMEM] * 3 + [IN_HBM] * 2 + [IN_VMEM],
        out_specs=[IN_VMEM] * 2,
        out_shape=[jax.ShapeDtypeStruct(lat.shape, BF16), jax.ShapeDtypeStruct(ids.shape, F32)],
        scratch_shapes=[pltpu.VMEM(masks.shape, BF16), pltpu.VMEM(spread.shape, BF16), pltpu.SemaphoreType.DMA((2,))],
        compiler_params=pltpu.CompilerParams(vmem_limit_bytes=32 * MIB),
        name="combine_back",
    )(ids, mix, lat, pinned(masks), pinned(spread), back)


def exchange(rows, owners):
    shape = rows.shape
    moved = lax.all_to_all(rows.reshape(owners, SUB, shape[1]), AXES, split_axis=0, concat_axis=0, tiled=True)
    return moved.reshape(shape)


def on_device(latent, grad_out, expert_ids, combine, w_up, w_down):
    owners = lax.axis_size("node") * lax.axis_size("local")
    experts = owners // 2 * w_up.shape[1]
    ids, mix = expert_ids.T, combine.T
    recv = exchange(pack(ids, mix, latent, grad_out, owners), owners)
    x, g, hg, sq, back = expert_rows(recv, jnp.swapaxes(w_up, 2, 3), w_down)
    returned = exchange(back, owners)
    d_up, d_down, masks, spread = weight_grads(ids, mix, hg, sq, x, g, experts)
    lat_grad, mix_grad = combine_back(ids, mix, latent, masks, spread, returned)
    return lat_grad, mix_grad.T, jnp.swapaxes(d_up, 1, 2)[None], d_down[None]


def solution(mesh):
    in_specs = (
        P(AXES, None),
        P(AXES, None),
        P(AXES, None),
        P(AXES, None),
        P(AXES, None, None, None),
        P(AXES, None, None, None),
    )
    out_specs = (
        P(AXES, None),
        P(AXES, None),
        P(AXES, None, None, None),
        P(AXES, None, None, None),
    )
    return jax.shard_map(
        on_device, mesh=mesh, in_specs=in_specs, out_specs=out_specs, check_vma=False
    )
```

```python
import functools

import jax
import jax.numpy as jnp
from jax import lax
from jax.experimental import pallas as pl
from jax.experimental.pallas import tpu as pltpu
from jax.sharding import PartitionSpec as P

F32 = jnp.float32
BF16 = jnp.bfloat16
CAP = 6
SUB = 8
GROUP = 256
MIB = 1 << 20
NN = (((1,), (0,)), ((), ()))
NT = (((1,), (1,)), ((), ()))
TN = (((0,), (0,)), ((), ()))
AXES = ("node", "local")
IN_HBM = pl.BlockSpec(memory_space=pltpu.HBM)
IN_VMEM = pl.BlockSpec(memory_space=pltpu.VMEM)


def dot(a, b, dims=NN):
    return lax.dot_general(a, b, dims, preferred_element_type=F32)


def iota(shape, dim):
    return lax.broadcasted_iota(jnp.int32, shape, dim)


def pinned(a):
    return pltpu.with_memory_space_constraint(a, pltpu.HBM)


def one_hot(mask):
    return jnp.where(mask, 1.0, 0.0).astype(BF16)


def pick_codes(ids, mix, experts):
    tokens = ids.shape[1]
    e_at = iota((experts, tokens), 0)
    hit = jnp.zeros((experts, tokens), F32)
    weight = jnp.zeros((experts, tokens), F32)
    for k in range(ids.shape[0]):
        named = ids[k : k + 1, :] == e_at
        hit = hit + jnp.where(named, 1.0, 0.0)
        weight = weight + jnp.where(named, mix[k : k + 1, :], 0.0)
    earlier = one_hot(iota((tokens, tokens), 0) < iota((tokens, tokens), 1))
    code = hit * (dot(hit.astype(BF16), earlier) + 1.0)
    return code.astype(BF16), weight.astype(BF16)


def slot_masks(code0, code1, s):
    main = jnp.where(s < CAP, code0 - 1, code1 + (CAP - 1)) == s
    main = main & (jnp.where(s < CAP, code0, code1) > 0)
    return main, (s < 4) & (code1 == s + 3), (s >= 4) & (code1 == s - 1)


def pack_kernel(ids_hbm, mix_hbm, lat_hbm, grad_hbm, out_ref, ids_s, mix_s, both_s, sems):
    tokens, width = lat_hbm.shape
    rows, experts = out_ref.shape[0], out_ref.shape[0] // SUB
    half, part = rows // 2, rows // 4
    loads = [
        pltpu.make_async_copy(hbm, to, sems.at[i])
        for i, (hbm, to) in enumerate(
            (
                (ids_hbm, ids_s),
                (mix_hbm, mix_s),
                (lat_hbm, both_s.at[pl.ds(0, tokens)]),
                (grad_hbm, both_s.at[pl.ds(tokens, tokens)]),
            )
        )
    ]
    for load in loads:
        load.start()
    at = iota((half, experts), 0) >> 3
    e_at = iota((half, experts), 1)
    even, odd = one_hot(e_at == 2 * at), one_hot(e_at == 2 * at + 1)
    s = iota((half, tokens), 0) & 7
    loads[0].wait()
    loads[1].wait()
    code, weight = pick_codes(ids_s[...], mix_s[...].astype(F32), experts)
    code0, code1 = dot(even, code).astype(jnp.int32), dot(odd, code).astype(jnp.int32)
    weight0, weight1 = dot(even, weight), dot(odd, weight)
    main, low, high = slot_masks(code0, code1, s)
    plain = one_hot(main)
    mixed = jnp.where(main, jnp.where(s < CAP, weight0, weight1), 0.0).astype(BF16)
    rest = jnp.concatenate([jnp.where(low, 1.0, 0.0), jnp.where(high, weight1, 0.0)], axis=1).astype(BF16)
    loads[2].wait()
    loads[3].wait()

    def twice(a):
        a = a.reshape(part // SUB, 1, SUB, width)
        return jnp.broadcast_to(a, (part // SUB, 2, SUB, width)).reshape(2 * part, width).astype(BF16)

    for i in range(2):
        here, to = slice(i * part, (i + 1) * part), slice(i * 2 * part, (i + 1) * 2 * part)
        out_ref[to, :width] = twice(dot(plain[here], both_s[:tokens, :]))
        out_ref[to, width : 2 * width] = twice(dot(mixed[here], both_s[tokens:, :]))
        out_ref[to, 2 * width :] = twice(dot(rest[here], both_s[...]))


def pack(ids, mix, lat, grad, owners):
    tokens, width = lat.shape
    rows = owners * SUB
    return pl.pallas_call(
        pack_kernel,
        in_specs=[IN_HBM] * 4,
        out_specs=IN_VMEM,
        out_shape=jax.ShapeDtypeStruct((rows, 3 * width), BF16),
        scratch_shapes=[
            pltpu.VMEM(ids.shape, jnp.int32),
            pltpu.VMEM(mix.shape, BF16),
            pltpu.VMEM((2 * tokens, width), BF16),
            pltpu.SemaphoreType.DMA((4,)),
        ],
        compiler_params=pltpu.CompilerParams(vmem_limit_bytes=24 * MIB),
        cost_estimate=pl.CostEstimate(flops=8 * rows * tokens * width, bytes_accessed=6 * rows * width, transcendentals=0),
        name="pack",
    )(pinned(ids), pinned(mix), pinned(lat), pinned(grad))


def slot_order(shape, pick_dim, tail):
    pick, row = iota(shape, pick_dim), iota(shape, 1 - pick_dim)
    source, s = row >> 3, row & 7
    if tail:
        half = GROUP // 2
        return one_hot(pick == jnp.where(s < 4, source * 4 + s, half + source * 4 + s - 4))
    first = GROUP // SUB * CAP
    return one_hot(pick == jnp.where(s < CAP, source * CAP + s, first + source * 2 + s - CAP))


def rows_kernel(
    recv_ref, up_ref, down_ref, x_hbm, g_hbm, hg_hbm, sq_hbm, back_hbm,
    x_s, g_s, hg_s, sq_s, y_s, back_s, sems, back_sems,
):
    exp_local, hidden, width = up_ref.shape[1:]
    half, quarter = width // 2, GROUP // 2
    groups = recv_ref.shape[0] // GROUP
    picks = x_s.shape[1]
    first = GROUP // SUB * CAP
    second = GROUP - first
    square = (GROUP, GROUP)
    kept = ((x_s, x_hbm), (g_s, g_hbm), (hg_s, hg_hbm), (sq_s, sq_hbm))

    def keep(which, j):
        scratch, hbm = kept[which]
        return pltpu.make_async_copy(scratch.at[j], hbm.at[j], sems.at[which, j])

    take, take_tail = slot_order(square, 0, False), slot_order(square, 0, True)

    def unfold(i, carry):
        raw = pl.ds(i * GROUP, GROUP)
        at = i * first
        whole, head, tail = pl.ds(at, first), pl.ds(at, second), pl.ds(at + second, quarter)
        for to, cols in ((x_s, slice(0, width)), (g_s, slice(width, 2 * width))):
            moved = dot(take, recv_ref[raw, cols]).astype(BF16)
            to[0, whole, :] = moved[:first]
            to[1, head, :] = moved[first:]
        moved = dot(take_tail, recv_ref[raw, 2 * width :]).astype(BF16)
        x_s[1, tail, :] = moved[:quarter]
        g_s[1, tail, :] = moved[quarter:]
        return carry

    for i in range(groups):
        unfold(i, 0)
    for j in range(exp_local):
        keep(0, j).start()
        keep(1, j).start()

    for j in range(exp_local):
        pre = dot(up_ref[0, j], x_s[j], NT)
        pulled = dot(down_ref[0, j], g_s[j], NT)
        act = jnp.maximum(pre, 0.0)
        sq_s[j] = (act * act).astype(BF16)
        hg_s[j] = (2.0 * act * pulled).astype(BF16)
        keep(2, j).start()
        keep(3, j).start()
        y_s[j] = dot(hg_s[j], up_ref[0, j], TN).astype(BF16)

    put, put_tail = slot_order(square, 1, False), slot_order(square, 1, True)

    def copy_out(i):
        raw = pl.ds(i * GROUP, GROUP)
        return pltpu.make_async_copy(back_s.at[raw], back_hbm.at[raw], back_sems.at[i])

    def fold(i, carry):
        raw = pl.ds(i * GROUP, GROUP)
        at = i * first
        whole, head, tail = pl.ds(at, first), pl.ds(at, second), pl.ds(at + second, quarter)
        main = jnp.concatenate([y_s[0, whole, :], y_s[1, head, :]], axis=0)
        back_s[raw, :width] = dot(put, main).astype(BF16)
        rest = jnp.concatenate([y_s[1, tail, :half], y_s[1, tail, half:]], axis=0)
        back_s[raw, width:] = dot(put_tail, rest).astype(BF16)
        copy_out(i).start()
        return carry

    for i in range(groups):
        fold(i, 0)
    for i in range(groups):
        copy_out(i).wait()
    for which in range(4):
        for j in range(exp_local):
            keep(which, j).wait()


def expert_rows(recv, up, down):
    rows = recv.shape[0]
    _, exp_local, hidden, width = up.shape
    picks = rows // SUB * CAP
    kept = [(exp_local, picks, width)] * 2 + [(exp_local, hidden, picks)] * 2
    back = (rows, 3 * width // 2)
    return pl.pallas_call(
        rows_kernel,
        in_specs=[IN_VMEM] * 3,
        out_specs=[IN_HBM] * 5,
        out_shape=[pltpu.HBM(shape, BF16) for shape in kept + [back]],
        scratch_shapes=[pltpu.VMEM(shape, BF16) for shape in kept + [kept[0], back]]
        + [pltpu.SemaphoreType.DMA(n) for n in ((4, exp_local), (rows // GROUP,))],
        compiler_params=pltpu.CompilerParams(vmem_limit_bytes=36 * MIB),
        cost_estimate=pl.CostEstimate(flops=6 * exp_local * picks * hidden * width, bytes_accessed=32 * MIB, transcendentals=0),
        name="expert_rows",
    )(recv, up, down)


def weights_kernel(experts, ids_ref, mix_ref, hg_ref, sq_ref, x_ref, g_ref, up_ref, down_ref, masks_ref, spread_ref):
    up_ref[0] = dot(hg_ref[0], x_ref[0]).astype(BF16)
    down_ref[0] = dot(sq_ref[0], g_ref[0]).astype(BF16)

    @pl.when((pl.program_id(0) == 0) & (pl.program_id(1) == 0))
    def _():
        tokens, rows = masks_ref.shape[1:]
        code, _ = pick_codes(ids_ref[...], mix_ref[...].astype(F32), experts)
        s = iota((tokens, rows), 1) & 7
        e_at, pair = iota((experts, rows), 0), 2 * (iota((experts, rows), 1) >> 4)
        even, odd = one_hot(e_at == pair), one_hot(e_at == pair + 1)
        code0 = dot(code, even, TN).astype(jnp.int32)
        code1 = dot(code, odd, TN).astype(jnp.int32)
        for i, mask in enumerate(slot_masks(code0, code1, s)):
            masks_ref[i] = one_hot(mask)
        spread_ref[0] = jnp.where((iota((experts, rows), 1) & 7) < CAP, even, odd)
        spread_ref[1] = odd


def weight_grads(ids, mix, hg, sq, x, g, experts, blocks=3):
    exp_local, hidden, picks = hg.shape
    width = x.shape[2]
    tokens, rows = ids.shape[1], picks // CAP * SUB
    hb = hidden // blocks
    whole = lambda a: pl.BlockSpec(a.shape, lambda j, i: (0,) * a.ndim)
    slab = pl.BlockSpec((1, hb, picks), lambda j, i: (j, i, 0))
    per_expert = pl.BlockSpec((1, picks, width), lambda j, i: (j, 0, 0))
    out = pl.BlockSpec((1, hb, width), lambda j, i: (j, i, 0))
    fixed = lambda n, m: pl.BlockSpec((n, m, rows), lambda j, i: (0, 0, 0))
    return pl.pallas_call(
        functools.partial(weights_kernel, experts),
        grid=(exp_local, blocks),
        in_specs=[whole(ids), whole(mix), slab, slab, per_expert, per_expert],
        out_specs=[out, out, fixed(3, tokens), fixed(2, experts)],
        out_shape=[jax.ShapeDtypeStruct((exp_local, hidden, width), BF16)] * 2
        + [pltpu.HBM((3, tokens, rows), BF16), pltpu.HBM((2, experts, rows), BF16)],
        compiler_params=pltpu.CompilerParams(vmem_limit_bytes=60 * MIB),
        cost_estimate=pl.CostEstimate(flops=4 * exp_local * picks * hidden * width, bytes_accessed=32 * MIB, transcendentals=0),
        name="weight_grads",
    )(ids, mix, hg, sq, x, g)


def combine_kernel(ids_ref, mix_ref, lat_ref, masks_hbm, spread_hbm, back_ref, lat_out, mix_out, masks_s, spread_s, sems):
    picks, tokens = ids_ref.shape
    experts = spread_s.shape[1]
    width = lat_ref.shape[1]
    half = width // 2
    load_masks = pltpu.make_async_copy(masks_hbm, masks_s, sems.at[0])
    load_spread = pltpu.make_async_copy(spread_hbm, spread_s, sems.at[1])
    load_masks.start()
    load_spread.start()
    tail = back_ref[:, width:]
    front_dots = dot(lat_ref[...], back_ref[:, :width], NT)
    tail_dots = dot(jnp.concatenate([lat_ref[:, :half], lat_ref[:, half:]], axis=0), tail, NT)
    load_masks.wait()
    main = masks_s[0]
    rest = jnp.concatenate([masks_s[1], masks_s[2]], axis=0)
    front_rows, tail_rows = dot(main, back_ref[:, :width]), dot(rest, tail)
    lat_out[:, :half] = (front_rows[:, :half] + tail_rows[:tokens]).astype(BF16)
    lat_out[:, half:] = (front_rows[:, half:] + tail_rows[tokens:]).astype(BF16)
    load_spread.wait()
    tail_dots = rest.astype(F32) * tail_dots
    gained = jnp.zeros((experts, 2 * tokens), F32)
    for i, dots in enumerate((main.astype(F32) * front_dots, tail_dots[:tokens] + tail_dots[tokens:])):
        upper = dots.astype(BF16)
        lower = (dots - upper.astype(F32)).astype(BF16)
        gained = gained + dot(spread_s[i], jnp.concatenate([upper, lower], axis=0), NT)
    gained = gained[:, :tokens] + gained[:, tokens:]
    e_at = iota((experts, tokens), 0)
    for k in range(picks):
        dots = jnp.sum(jnp.where(ids_ref[k : k + 1, :] == e_at, gained, 0.0), axis=0, keepdims=True)
        mix_out[k : k + 1, :] = dots / (2.0 * mix_ref[k : k + 1, :].astype(F32))


def combine_back(ids, mix, lat, masks, spread, back):
    return pl.pallas_call(
        combine_kernel,
        in_specs=[IN_VMEM] * 3 + [IN_HBM] * 2 + [IN_VMEM],
        out_specs=[IN_VMEM] * 2,
        out_shape=[jax.ShapeDtypeStruct(lat.shape, BF16), jax.ShapeDtypeStruct(ids.shape, F32)],
        scratch_shapes=[pltpu.VMEM(masks.shape, BF16), pltpu.VMEM(spread.shape, BF16), pltpu.SemaphoreType.DMA((2,))],
        compiler_params=pltpu.CompilerParams(vmem_limit_bytes=32 * MIB),
        name="combine_back",
    )(ids, mix, lat, pinned(masks), pinned(spread), back)


def exchange(rows, owners):
    shape = rows.shape
    moved = lax.all_to_all(rows.reshape(owners, SUB, shape[1]), AXES, split_axis=0, concat_axis=0, tiled=True)
    return moved.reshape(shape)


def on_device(latent, grad_out, expert_ids, combine, w_up, w_down):
    owners = lax.axis_size("node") * lax.axis_size("local")
    experts = owners // 2 * w_up.shape[1]
    ids, mix = expert_ids.T, combine.T
    recv = exchange(pack(ids, mix, latent, grad_out, owners), owners)
    x, g, hg, sq, back = expert_rows(recv, jnp.swapaxes(w_up, 2, 3), w_down)
    returned = exchange(back, owners)
    d_up, d_down, masks, spread = weight_grads(ids, mix, hg, sq, x, g, experts)
    lat_grad, mix_grad = combine_back(ids, mix, latent, masks, spread, returned)
    return lat_grad, mix_grad.T, jnp.swapaxes(d_up, 1, 2)[None], d_down[None]


def solution(mesh):
    in_specs = (
        P(AXES, None),
        P(AXES, None),
        P(AXES, None),
        P(AXES, None),
        P(AXES, None, None, None),
        P(AXES, None, None, None),
    )
    out_specs = (
        P(AXES, None),
        P(AXES, None),
        P(AXES, None, None, None),
        P(AXES, None, None, None),
    )
    return jax.shard_map(
        on_device, mesh=mesh, in_specs=in_specs, out_specs=out_specs, check_vma=False
    )
```

```python
import functools

import jax
import jax.numpy as jnp
from jax import lax
from jax.experimental import pallas as pl
from jax.experimental.pallas import tpu as pltpu
from jax.sharding import PartitionSpec as P

F32 = jnp.float32
BF16 = jnp.bfloat16
CAP = 6
SUB = 8
GROUP = 256
MIB = 1 << 20
NN = (((1,), (0,)), ((), ()))
NT = (((1,), (1,)), ((), ()))
TN = (((0,), (0,)), ((), ()))
AXES = ("node", "local")
IN_HBM = pl.BlockSpec(memory_space=pltpu.HBM)
IN_VMEM = pl.BlockSpec(memory_space=pltpu.VMEM)


def dot(a, b, dims=NN):
    return lax.dot_general(a, b, dims, preferred_element_type=F32)


def iota(shape, dim):
    return lax.broadcasted_iota(jnp.int32, shape, dim)


def pinned(a):
    return pltpu.with_memory_space_constraint(a, pltpu.HBM)


def one_hot(mask):
    return jnp.where(mask, 1.0, 0.0).astype(BF16)


def pick_codes(ids, mix, experts):
    tokens = ids.shape[1]
    e_at = iota((experts, tokens), 0)
    hit = jnp.zeros((experts, tokens), F32)
    weight = jnp.zeros((experts, tokens), F32)
    for k in range(ids.shape[0]):
        named = ids[k : k + 1, :] == e_at
        hit = hit + jnp.where(named, 1.0, 0.0)
        weight = weight + jnp.where(named, mix[k : k + 1, :], 0.0)
    earlier = one_hot(iota((tokens, tokens), 0) < iota((tokens, tokens), 1))
    code = hit * (dot(hit.astype(BF16), earlier) + 1.0)
    return code.astype(BF16), weight.astype(BF16)


def slot_masks(code0, code1, s):
    main = jnp.where(s < CAP, code0 - 1, code1 + (CAP - 1)) == s
    main = main & (jnp.where(s < CAP, code0, code1) > 0)
    return main, (s < 4) & (code1 == s + 3), (s >= 4) & (code1 == s - 1)


def pack_kernel(ids_hbm, mix_hbm, lat_hbm, grad_hbm, out_ref, ids_s, mix_s, both_s, sems):
    tokens, width = lat_hbm.shape
    rows, experts = out_ref.shape[0], out_ref.shape[0] // SUB
    half, part = rows // 2, rows // 4
    loads = [
        pltpu.make_async_copy(hbm, to, sems.at[i])
        for i, (hbm, to) in enumerate(
            (
                (ids_hbm, ids_s),
                (mix_hbm, mix_s),
                (lat_hbm, both_s.at[pl.ds(0, tokens)]),
                (grad_hbm, both_s.at[pl.ds(tokens, tokens)]),
            )
        )
    ]
    for load in loads:
        load.start()
    at = iota((half, experts), 0) >> 3
    e_at = iota((half, experts), 1)
    even, odd = one_hot(e_at == 2 * at), one_hot(e_at == 2 * at + 1)
    s = iota((half, tokens), 0) & 7
    loads[0].wait()
    loads[1].wait()
    code, weight = pick_codes(ids_s[...], mix_s[...].astype(F32), experts)
    code0, code1 = dot(even, code).astype(jnp.int32), dot(odd, code).astype(jnp.int32)
    weight0, weight1 = dot(even, weight), dot(odd, weight)
    main, low, high = slot_masks(code0, code1, s)
    plain = one_hot(main)
    mixed = jnp.where(main, jnp.where(s < CAP, weight0, weight1), 0.0).astype(BF16)
    rest = jnp.concatenate([jnp.where(low, 1.0, 0.0), jnp.where(high, weight1, 0.0)], axis=1).astype(BF16)
    loads[2].wait()
    loads[3].wait()

    def twice(a):
        a = a.reshape(part // SUB, 1, SUB, width)
        return jnp.broadcast_to(a, (part // SUB, 2, SUB, width)).reshape(2 * part, width).astype(BF16)

    for i in range(2):
        here, to = slice(i * part, (i + 1) * part), slice(i * 2 * part, (i + 1) * 2 * part)
        out_ref[to, :width] = twice(dot(plain[here], both_s[:tokens, :]))
        out_ref[to, width : 2 * width] = twice(dot(mixed[here], both_s[tokens:, :]))
        out_ref[to, 2 * width :] = twice(dot(rest[here], both_s[...]))


def pack(ids, mix, lat, grad, owners):
    tokens, width = lat.shape
    rows = owners * SUB
    return pl.pallas_call(
        pack_kernel,
        in_specs=[IN_HBM] * 4,
        out_specs=IN_VMEM,
        out_shape=jax.ShapeDtypeStruct((rows, 3 * width), BF16),
        scratch_shapes=[
            pltpu.VMEM(ids.shape, jnp.int32),
            pltpu.VMEM(mix.shape, BF16),
            pltpu.VMEM((2 * tokens, width), BF16),
            pltpu.SemaphoreType.DMA((4,)),
        ],
        compiler_params=pltpu.CompilerParams(vmem_limit_bytes=24 * MIB),
        cost_estimate=pl.CostEstimate(flops=8 * rows * tokens * width, bytes_accessed=6 * rows * width, transcendentals=0),
        name="pack",
    )(pinned(ids), pinned(mix), pinned(lat), pinned(grad))


def slot_order(shape, pick_dim, tail):
    pick, row = iota(shape, pick_dim), iota(shape, 1 - pick_dim)
    source, s = row >> 3, row & 7
    if tail:
        half = GROUP // 2
        return one_hot(pick == jnp.where(s < 4, source * 4 + s, half + source * 4 + s - 4))
    first = GROUP // SUB * CAP
    return one_hot(pick == jnp.where(s < CAP, source * CAP + s, first + source * 2 + s - CAP))


def rows_kernel(
    recv_ref, up_ref, down_ref, x_hbm, g_hbm, hg_hbm, sq_hbm, back_hbm,
    x_s, g_s, hg_s, sq_s, y_s, back_s, sems, back_sems,
):
    exp_local, hidden, width = up_ref.shape[1:]
    half, quarter = width // 2, GROUP // 2
    groups = recv_ref.shape[0] // GROUP
    picks = x_s.shape[1]
    first = GROUP // SUB * CAP
    second = GROUP - first
    square = (GROUP, GROUP)
    kept = ((x_s, x_hbm), (g_s, g_hbm), (hg_s, hg_hbm), (sq_s, sq_hbm))

    def keep(which, j):
        scratch, hbm = kept[which]
        return pltpu.make_async_copy(scratch.at[j], hbm.at[j], sems.at[which, j])

    take, take_tail = slot_order(square, 0, False), slot_order(square, 0, True)

    def unfold(i, carry):
        raw = pl.ds(i * GROUP, GROUP)
        at = i * first
        whole, head, tail = pl.ds(at, first), pl.ds(at, second), pl.ds(at + second, quarter)
        for to, cols in ((x_s, slice(0, width)), (g_s, slice(width, 2 * width))):
            moved = dot(take, recv_ref[raw, cols]).astype(BF16)
            to[0, whole, :] = moved[:first]
            to[1, head, :] = moved[first:]
        moved = dot(take_tail, recv_ref[raw, 2 * width :]).astype(BF16)
        x_s[1, tail, :] = moved[:quarter]
        g_s[1, tail, :] = moved[quarter:]
        return carry

    for i in range(groups):
        unfold(i, 0)
    for j in range(exp_local):
        keep(0, j).start()
        keep(1, j).start()

    acts, pulls = [], []
    for j in range(exp_local):
        acts.append(dot(up_ref[0, j], x_s[j], NT))
        pulls.append(dot(down_ref[0, j], g_s[j], NT))
    for j in range(exp_local):
        act = jnp.maximum(acts[j], 0.0)
        sq_s[j] = (act * act).astype(BF16)
        hg_s[j] = (2.0 * act * pulls[j]).astype(BF16)
        keep(2, j).start()
        keep(3, j).start()
        y_s[j] = dot(hg_s[j], up_ref[0, j], TN).astype(BF16)

    put, put_tail = slot_order(square, 1, False), slot_order(square, 1, True)

    def copy_out(i):
        raw = pl.ds(i * GROUP, GROUP)
        return pltpu.make_async_copy(back_s.at[raw], back_hbm.at[raw], back_sems.at[i])

    def fold(i, carry):
        raw = pl.ds(i * GROUP, GROUP)
        at = i * first
        whole, head, tail = pl.ds(at, first), pl.ds(at, second), pl.ds(at + second, quarter)
        main = jnp.concatenate([y_s[0, whole, :], y_s[1, head, :]], axis=0)
        back_s[raw, :width] = dot(put, main).astype(BF16)
        rest = jnp.concatenate([y_s[1, tail, :half], y_s[1, tail, half:]], axis=0)
        back_s[raw, width:] = dot(put_tail, rest).astype(BF16)
        copy_out(i).start()
        return carry

    for i in range(groups):
        fold(i, 0)
    for i in range(groups):
        copy_out(i).wait()
    for which in range(4):
        for j in range(exp_local):
            keep(which, j).wait()


def expert_rows(recv, up, down):
    rows = recv.shape[0]
    _, exp_local, hidden, width = up.shape
    picks = rows // SUB * CAP
    kept = [(exp_local, picks, width)] * 2 + [(exp_local, hidden, picks)] * 2
    back = (rows, 3 * width // 2)
    return pl.pallas_call(
        rows_kernel,
        in_specs=[IN_VMEM] * 3,
        out_specs=[IN_HBM] * 5,
        out_shape=[pltpu.HBM(shape, BF16) for shape in kept + [back]],
        scratch_shapes=[pltpu.VMEM(shape, BF16) for shape in kept + [kept[0], back]]
        + [pltpu.SemaphoreType.DMA(n) for n in ((4, exp_local), (rows // GROUP,))],
        compiler_params=pltpu.CompilerParams(vmem_limit_bytes=36 * MIB),
        cost_estimate=pl.CostEstimate(flops=6 * exp_local * picks * hidden * width, bytes_accessed=32 * MIB, transcendentals=0),
        name="expert_rows",
    )(recv, up, down)


def weights_kernel(experts, ids_ref, mix_ref, hg_ref, sq_ref, x_ref, g_ref, up_ref, down_ref, masks_ref, spread_ref):
    up_ref[0] = dot(hg_ref[0], x_ref[0]).astype(BF16)
    down_ref[0] = dot(sq_ref[0], g_ref[0]).astype(BF16)

    @pl.when((pl.program_id(0) == 0) & (pl.program_id(1) == 0))
    def _():
        tokens, rows = masks_ref.shape[1:]
        code, _ = pick_codes(ids_ref[...], mix_ref[...].astype(F32), experts)
        s = iota((tokens, rows), 1) & 7
        e_at, pair = iota((experts, rows), 0), 2 * (iota((experts, rows), 1) >> 4)
        even, odd = one_hot(e_at == pair), one_hot(e_at == pair + 1)
        code0 = dot(code, even, TN).astype(jnp.int32)
        code1 = dot(code, odd, TN).astype(jnp.int32)
        for i, mask in enumerate(slot_masks(code0, code1, s)):
            masks_ref[i] = one_hot(mask)
        spread_ref[0] = jnp.where((iota((experts, rows), 1) & 7) < CAP, even, odd)
        spread_ref[1] = odd


def weight_grads(ids, mix, hg, sq, x, g, experts, blocks=3):
    exp_local, hidden, picks = hg.shape
    width = x.shape[2]
    tokens, rows = ids.shape[1], picks // CAP * SUB
    hb = hidden // blocks
    whole = lambda a: pl.BlockSpec(a.shape, lambda j, i: (0,) * a.ndim)
    slab = pl.BlockSpec((1, hb, picks), lambda j, i: (j, i, 0))
    per_expert = pl.BlockSpec((1, picks, width), lambda j, i: (j, 0, 0))
    out = pl.BlockSpec((1, hb, width), lambda j, i: (j, i, 0))
    fixed = lambda n, m: pl.BlockSpec((n, m, rows), lambda j, i: (0, 0, 0))
    return pl.pallas_call(
        functools.partial(weights_kernel, experts),
        grid=(exp_local, blocks),
        in_specs=[whole(ids), whole(mix), slab, slab, per_expert, per_expert],
        out_specs=[out, out, fixed(3, tokens), fixed(2, experts)],
        out_shape=[jax.ShapeDtypeStruct((exp_local, hidden, width), BF16)] * 2
        + [pltpu.HBM((3, tokens, rows), BF16), pltpu.HBM((2, experts, rows), BF16)],
        compiler_params=pltpu.CompilerParams(vmem_limit_bytes=60 * MIB),
        cost_estimate=pl.CostEstimate(flops=4 * exp_local * picks * hidden * width, bytes_accessed=32 * MIB, transcendentals=0),
        name="weight_grads",
    )(ids, mix, hg, sq, x, g)


def combine_kernel(ids_ref, mix_ref, lat_ref, masks_hbm, spread_hbm, back_ref, lat_out, mix_out, masks_s, spread_s, sems):
    picks, tokens = ids_ref.shape
    experts = spread_s.shape[1]
    width = lat_ref.shape[1]
    half = width // 2
    load_masks = pltpu.make_async_copy(masks_hbm, masks_s, sems.at[0])
    load_spread = pltpu.make_async_copy(spread_hbm, spread_s, sems.at[1])
    load_masks.start()
    load_spread.start()
    tail = back_ref[:, width:]
    front_dots = dot(lat_ref[...], back_ref[:, :width], NT)
    tail_dots = dot(jnp.concatenate([lat_ref[:, :half], lat_ref[:, half:]], axis=0), tail, NT)
    load_masks.wait()
    main = masks_s[0]
    rest = jnp.concatenate([masks_s[1], masks_s[2]], axis=0)
    front_rows, tail_rows = dot(main, back_ref[:, :width]), dot(rest, tail)
    lat_out[:, :half] = (front_rows[:, :half] + tail_rows[:tokens]).astype(BF16)
    lat_out[:, half:] = (front_rows[:, half:] + tail_rows[tokens:]).astype(BF16)
    load_spread.wait()
    tail_dots = rest.astype(F32) * tail_dots
    gained = jnp.zeros((experts, 2 * tokens), F32)
    for i, dots in enumerate((main.astype(F32) * front_dots, tail_dots[:tokens] + tail_dots[tokens:])):
        upper = dots.astype(BF16)
        lower = (dots - upper.astype(F32)).astype(BF16)
        gained = gained + dot(spread_s[i], jnp.concatenate([upper, lower], axis=0), NT)
    gained = gained[:, :tokens] + gained[:, tokens:]
    e_at = iota((experts, tokens), 0)
    for k in range(picks):
        dots = jnp.sum(jnp.where(ids_ref[k : k + 1, :] == e_at, gained, 0.0), axis=0, keepdims=True)
        mix_out[k : k + 1, :] = dots / (2.0 * mix_ref[k : k + 1, :].astype(F32))


def combine_back(ids, mix, lat, masks, spread, back):
    return pl.pallas_call(
        combine_kernel,
        in_specs=[IN_VMEM] * 3 + [IN_HBM] * 2 + [IN_VMEM],
        out_specs=[IN_VMEM] * 2,
        out_shape=[jax.ShapeDtypeStruct(lat.shape, BF16), jax.ShapeDtypeStruct(ids.shape, F32)],
        scratch_shapes=[pltpu.VMEM(masks.shape, BF16), pltpu.VMEM(spread.shape, BF16), pltpu.SemaphoreType.DMA((2,))],
        compiler_params=pltpu.CompilerParams(vmem_limit_bytes=32 * MIB),
        name="combine_back",
    )(ids, mix, lat, pinned(masks), pinned(spread), back)


def exchange(rows, owners):
    shape = rows.shape
    moved = lax.all_to_all(rows.reshape(owners, SUB, shape[1]), AXES, split_axis=0, concat_axis=0, tiled=True)
    return moved.reshape(shape)


def on_device(latent, grad_out, expert_ids, combine, w_up, w_down):
    owners = lax.axis_size("node") * lax.axis_size("local")
    experts = owners // 2 * w_up.shape[1]
    ids, mix = expert_ids.T, combine.T
    recv = exchange(pack(ids, mix, latent, grad_out, owners), owners)
    x, g, hg, sq, back = expert_rows(recv, jnp.swapaxes(w_up, 2, 3), w_down)
    returned = exchange(back, owners)
    d_up, d_down, masks, spread = weight_grads(ids, mix, hg, sq, x, g, experts)
    lat_grad, mix_grad = combine_back(ids, mix, latent, masks, spread, returned)
    return lat_grad, mix_grad.T, jnp.swapaxes(d_up, 1, 2)[None], d_down[None]


def solution(mesh):
    in_specs = (
        P(AXES, None),
        P(AXES, None),
        P(AXES, None),
        P(AXES, None),
        P(AXES, None, None, None),
        P(AXES, None, None, None),
    )
    out_specs = (
        P(AXES, None),
        P(AXES, None),
        P(AXES, None, None, None),
        P(AXES, None, None, None),
    )
    return jax.shard_map(
        on_device, mesh=mesh, in_specs=in_specs, out_specs=out_specs, check_vma=False
    )
```
